32 devices in a mesh: block: 8 (over z, x), grp: 4 (over y, core).
Axes of the slice: x: 2, y: 2, z: 4, core: 2. Of those that a mesh axis runs over, the one named last changes fastest.
Arguments:
- features: bfloat16 [128, 256, 128], P(('block', 'grp')), may hold values from -6 to 6
- point_counts: int32 [128], P(('block', 'grp')), may hold values from 128 to 256, as said below
- kernel_weights: bfloat16 [15, 128, 128], replicated, may hold values from -0.015625 to 0.015625
- influence: bfloat16 [256, 15, 256, 256], P(('block', 'grp')), may hold values from 0 to 1
- pair_list: int32 [256, 2], P(('block', 'grp')), may hold values from 0 to 127, as said below
- pair_counts: int32 [32], P(('block', 'grp')), may hold values from 1 to 8, as said below
- cotangent: bfloat16 [128, 256, 128], P(('block', 'grp')), may hold values from -6 to 6
Outputs:
- activated: bfloat16 [128, 256, 128], P(('block', 'grp'))
- grad_features: bfloat16 [128, 256, 128], P(('block', 'grp'))
- grad_weights: float32 [15, 128, 128], replicated
The draws below stay inside these ranges and needn't reach their ends.
Inputs may be any that keep to these rules, and one draw needn't show every extreme that they name: `pair_list`: block x lives on device x // 4, and device d has block index d // 4 and grp index d % 4. Column 0 is below 4; the second block of every slot lives on a device whose block index differs from the slot's device's by at most one; any grp index may occur. `pair_counts`: slots at or beyond a device's count are unused. Some device uses all 8 slots. `point_counts`: the real points of a block are its first rows; the others are padding.
All inputs are finite; a program needn't handle non-finite values.
Results may differ from the reference program's by a relative error of at most 0.0063.
Values may be sent and summed in bfloat16 or wider, within the bound.
A program may use at most 128 MiB of HBM per device.

```python
import math
import jax
import jax.numpy as jnp
from jax import lax

C = 128
K = 15
P_SIZE = 256
BLK_DEV = 4
PAIR_DEV = 8
BLOCKS = 128
SLOTS = 256
POINTS = 32768
N_BLOCK = 8
N_GRP = 4


def draw_pair_list(key, part):
    total = N_BLOCK * N_GRP * PAIR_DEV
    keys = jax.random.split(key, 4)
    device = jnp.arange(total, dtype=jnp.int32) // PAIR_DEV
    column = device // N_GRP
    first = jax.random.randint(keys[0], (total,), 0, BLK_DEV, dtype=jnp.int32)
    offset = jax.random.randint(keys[1], (total,), -1, 2, dtype=jnp.int32)
    target = jnp.clip(column + offset, 0, N_BLOCK - 1)
    region = jax.random.randint(keys[2], (total,), 0, N_GRP, dtype=jnp.int32)
    local = jax.random.randint(keys[3], (total,), 0, BLK_DEV, dtype=jnp.int32)
    second = (target * N_GRP + region) * BLK_DEV + local
    return jnp.stack([first, second], axis=1).astype(jnp.int32)


def draw_pair_counts(key, part):
    devices_all = N_BLOCK * N_GRP
    keys = jax.random.split(key, 3)
    base = jax.random.randint(keys[0], (devices_all,), min(3, PAIR_DEV), min(6, PAIR_DEV) + 1, dtype=jnp.int32)
    busy = jax.random.randint(keys[1], (devices_all,), 0, 8, dtype=jnp.int32) == 0
    chosen = jax.random.randint(keys[2], (), 0, devices_all, dtype=jnp.int32)
    forced = jnp.arange(devices_all, dtype=jnp.int32) == chosen
    return jnp.where(busy | forced, PAIR_DEV, base).astype(jnp.int32)


def draw_point_counts(key, part):
    keys = jax.random.split(key, 3)
    counts = jax.random.randint(keys[0], (BLOCKS,), P_SIZE // 2, P_SIZE + 1, dtype=jnp.int32)
    full_at = jax.random.randint(keys[1], (), 0, BLOCKS, dtype=jnp.int32)
    half_at = (full_at + 1 + jax.random.randint(keys[2], (), 0, BLOCKS - 1, dtype=jnp.int32)) % BLOCKS
    index = jnp.arange(BLOCKS, dtype=jnp.int32)
    counts = jnp.where(index == full_at, P_SIZE, counts)
    counts = jnp.where(index == half_at, P_SIZE // 2, counts)
    return counts.astype(jnp.int32)


def steps_of(key, shape, pieces, least, largest):
    def one(axis_at, blocks):
        draws = jax.random.uniform(jax.random.fold_in(jax.random.fold_in(key, 6), axis_at), (blocks,), jnp.float32, least / len(pieces), largest / len(pieces))
        return jnp.repeat(jnp.exp(draws), shape[axis_at] // blocks).reshape((-1,) + (1,) * (len(shape) - axis_at - 1))

    level = one(*pieces[0])
    for cut in pieces[1:]:
        level = level * one(*cut)
    return level


def bell_draw(own_key, extent, spread, limit, cuts=(), kind=jnp.bfloat16):
    values = jax.random.normal(own_key, extent, jnp.float32) * spread
    if len(cuts) > 0:
        values = steps_of(own_key, extent, cuts, -0.22, 0.18) * values
    return jnp.clip(values, min=-limit, max=limit).astype(kind)


def setup_inputs(seed: int = 0) -> dict:
    key_list = jax.random.split(jax.random.key(seed), 8)
    features = bell_draw(key_list[0], (BLOCKS, P_SIZE, C), 1.0, 6.0, ((0, 32),))
    point_counts = draw_point_counts(jax.random.fold_in(key_list[7], 71), 0)
    kernel_weights = bell_draw(key_list[2], (K, C, C), (K * C * P_SIZE // 3) ** -0.5, 0.015625)
    influence = jnp.clip(1.0 * jax.random.uniform(key_list[3], (SLOTS, K, P_SIZE, P_SIZE), jnp.float32) ** steps_of(key_list[3], (SLOTS, K, P_SIZE, P_SIZE), ((0, 32),), -0.2, 0.2), 0.0, 1.0).astype(jnp.bfloat16)
    pair_list = draw_pair_list(jax.random.fold_in(key_list[7], 71), 0)
    pair_counts = draw_pair_counts(jax.random.fold_in(key_list[7], 71), 0)
    cotangent = bell_draw(key_list[6], (BLOCKS, P_SIZE, C), 1.0, 6.0, ((0, 32),))
    return dict(features=features, point_counts=point_counts, kernel_weights=kernel_weights, influence=influence, pair_list=pair_list, pair_counts=pair_counts, cotangent=cotangent)


def gather_terms(tile, rows):
    out = jnp.einsum('kij,jc->ikc', tile.astype(jnp.float32), rows.astype(jnp.float32))
    return out.astype(jnp.bfloat16).reshape(P_SIZE, K * C)

def scatter_terms(tile, rows):
    out = jnp.einsum('kij,ic->jkc', tile.astype(jnp.float32), rows.astype(jnp.float32))
    return out.astype(jnp.bfloat16).reshape(P_SIZE, K * C)

def reference(features, point_counts, kernel_weights, influence, pair_list, pair_counts, cotangent):
    valid = (jnp.arange(P_SIZE, dtype=jnp.int32)[None, :] < point_counts[:, None])[..., None]
    masked = jnp.where(valid, features, jnp.zeros_like(features))
    direct = kernel_weights.reshape(K * C, C)
    mirrored = kernel_weights[::-1].reshape(K * C, C)
    slot_ids = jnp.arange(SLOTS, dtype=jnp.int32)

    def locate(pair, slot):
        device = (slot // PAIR_DEV).astype(jnp.int32)
        active = slot - device * PAIR_DEV < pair_counts[device]
        first = (device * BLK_DEV + pair[0]).astype(jnp.int32)
        second = pair[1].astype(jnp.int32)
        return (active, first, second)

    def forward(total, item):
        tile, pair, slot = item
        active, first, second = locate(pair, slot)

        def work(total):
            to_first = jnp.dot(gather_terms(tile, masked[second]), direct, preferred_element_type=jnp.float32)
            to_second = jnp.dot(scatter_terms(tile, masked[first]), mirrored, preferred_element_type=jnp.float32)
            total = total.at[first].add(to_first)
            return total.at[second].add(to_second)
        return (lax.cond(active, work, lambda total: total, total), None)
    start = jnp.zeros((BLOCKS, P_SIZE, C), jnp.float32)
    total, _ = lax.scan(forward, start, (influence, pair_list, slot_ids))
    pre = jnp.where(valid, total, jnp.zeros_like(total))
    activated = jax.nn.silu(pre).astype(jnp.bfloat16)
    sig = jax.nn.sigmoid(pre)
    slope = sig * (1.0 + pre * (1.0 - sig))
    upstream = jnp.where(valid, cotangent.astype(jnp.float32) * slope, jnp.zeros_like(pre)).astype(jnp.bfloat16)

    def backward(carry, item):
        tile, pair, slot = item
        active, first, second = locate(pair, slot)

        def work(carry):
            grad_rows, grad_direct, grad_mirror = carry
            near_terms = gather_terms(tile, masked[second])
            own_terms = scatter_terms(tile, masked[first])
            up_first = upstream[first]
            up_second = upstream[second]
            grad_direct = grad_direct + jnp.dot(near_terms.T, up_first, preferred_element_type=jnp.float32)
            grad_mirror = grad_mirror + jnp.dot(own_terms.T, up_second, preferred_element_type=jnp.float32)
            back_near = jnp.dot(up_first, direct.T, preferred_element_type=jnp.float32).astype(jnp.bfloat16).reshape(P_SIZE, K, C)
            back_own = jnp.dot(up_second, mirrored.T, preferred_element_type=jnp.float32).astype(jnp.bfloat16).reshape(P_SIZE, K, C)
            to_second = jnp.einsum('kij,ikc->jc', tile.astype(jnp.float32), back_near.astype(jnp.float32))
            to_first = jnp.einsum('kij,jkc->ic', tile.astype(jnp.float32), back_own.astype(jnp.float32))
            grad_rows = grad_rows.at[second].add(to_second)
            grad_rows = grad_rows.at[first].add(to_first)
            return (grad_rows, grad_direct, grad_mirror)
        return (lax.cond(active, work, lambda carry: carry, carry), None)
    empty = jnp.zeros((K * C, C), jnp.float32)
    carry, _ = lax.scan(backward, (start, empty, empty), (influence, pair_list, slot_ids))
    grad_rows, grad_direct, grad_mirror = carry
    grad_features = jnp.where(valid, grad_rows, jnp.zeros_like(grad_rows)).astype(jnp.bfloat16)
    grad_weights = (grad_direct.reshape(K, C, C) + grad_mirror.reshape(K, C, C)[::-1]) * (1.0 / math.sqrt(POINTS))
    return (activated, grad_features, grad_weights)
```

```python
import functools
import math

import jax
import jax.numpy as jnp
from jax import lax
from jax.experimental import pallas as pl
from jax.experimental.pallas import tpu as pltpu
from jax.sharding import PartitionSpec as P

MESH = pl.DeviceIdType.MESH
F32, BF16 = jnp.float32, jnp.bfloat16
VMEM_BYTES = 56 * 2**20
PARTS = 2
VMEM = pl.BlockSpec(memory_space=pltpu.VMEM)
SMEM = pl.BlockSpec(memory_space=pltpu.SMEM)


def low_bit(mask):
    return mask & -mask


def grp_masks(groups):
    return sorted(range(1, groups), key=lambda m: (-low_bit(m), m))


def grp_bits(groups):
    return [1 << i for i in reversed(range(groups.bit_length() - 1))]


def where_am_i(columns):
    b, g = lax.axis_index("block"), lax.axis_index("grp")
    return b, g, {0: b > 0, 1: None, 2: b < columns - 1}


def under(condition, action):
    if condition is None:
        action()
    else:
        pl.when(condition)(action)


def greet(columns, groups):
    b, g, has = where_am_i(columns)
    barrier = pltpu.get_barrier_semaphore()
    for bit in grp_bits(groups):
        pl.semaphore_signal(barrier, inc=1, device_id=(b, g ^ bit), device_id_type=MESH)
    for side, step in ((0, -1), (2, 1)):
        @pl.when(has[side])
        def _():
            pl.semaphore_signal(barrier, inc=1, device_id=(b + step, g), device_id_type=MESH)
    peers = len(grp_bits(groups)) + has[0].astype(jnp.int32) + has[2].astype(jnp.int32)
    pl.semaphore_wait(barrier, peers)


def spread(near, send_sem, recv_sem, columns):
    b, g, has = where_am_i(columns)
    groups, blocks = near.shape[1], near.shape[2]
    span = blocks // PARTS
    opposite = {0: 2, 2: 0}

    def at(col, mask, part):
        return near.at[col, g ^ mask, pl.ds(part * span, span)]

    def sem(col, mask, part):
        return (col * groups + mask) * PARTS + part

    def side_copy(col, part):
        i = sem(col, 0, part)
        step = 1 if col == 0 else -1
        return pltpu.make_async_remote_copy(
            src_ref=at(1, 0, part), dst_ref=at(col, 0, part), send_sem=send_sem.at[i],
            recv_sem=recv_sem.at[i], device_id=(b + step, g), device_id_type=MESH)

    def grp_copy(col, mask, part):
        bit = low_bit(mask)
        i = sem(col, mask, part)
        return pltpu.make_async_remote_copy(
            src_ref=at(col, mask ^ bit, part), dst_ref=at(col, mask ^ bit, part), send_sem=send_sem.at[i],
            recv_sem=recv_sem.at[i], device_id=(b, g ^ bit), device_id_type=MESH)

    def arrival(col, mask, part):
        bit = low_bit(mask)
        i = sem(col, mask, part)
        return pltpu.make_async_remote_copy(
            src_ref=at(col, mask ^ bit, part), dst_ref=at(col, mask, part), send_sem=send_sem.at[i],
            recv_sem=recv_sem.at[i], device_id=(b, g ^ bit), device_id_type=MESH)

    def forward(col, mask, part):
        for bit in grp_bits(groups):
            if mask == 0 or bit < low_bit(mask):
                grp_copy(col, mask | bit, part).start()

    parts = range(PARTS)
    for part in parts:
        for col in (0, 2):
            pl.when(has[opposite[col]])(lambda: side_copy(col, part).start())
        forward(1, 0, part)
    for part in parts:
        for col in (0, 2):
            @pl.when(has[col])
            def _():
                side_copy(col, part).wait_recv()
                forward(col, 0, part)
    masks = grp_masks(groups)
    for mask in masks:
        for part in parts:
            for col in (1, 0, 2):
                def step():
                    arrival(col, mask, part).wait_recv()
                    forward(col, mask, part)
                under(has[col], step)
    for part in parts:
        for col in (0, 2):
            pl.when(has[opposite[col]])(lambda: side_copy(col, part).wait_send())
    for mask in masks:
        for part in parts:
            for col in (0, 1, 2):
                under(has[col], lambda: grp_copy(col, mask, part).wait_send())


def add_blocks(out, one, two, span):
    for i in range(span):
        out[i] = (one[i].astype(F32) + two[i].astype(F32)).astype(BF16)


def gather_back(sent, acc, land, beside, send_sem, recv_sem, columns):
    b, g, has = where_am_i(columns)
    groups, blocks = sent.shape[1], sent.shape[2]
    span = blocks // PARTS
    opposite = {0: 2, 2: 0}
    cols = (0, 2, 1)
    parts = range(PARTS)
    masks = grp_masks(groups)

    def cut(part):
        return pl.ds(part * span, span)

    def sem(col, mask, part):
        return (col * groups + mask) * PARTS + part

    def grp_copy(col, mask, part):
        bit = low_bit(mask)
        i = sem(col, mask, part)
        src = sent.at[col, g ^ mask, cut(part)] if bit == 1 else acc.at[col, mask, cut(part)]
        return pltpu.make_async_remote_copy(
            src_ref=src, dst_ref=land.at[col, mask, cut(part)], send_sem=send_sem.at[i],
            recv_sem=recv_sem.at[i], device_id=(b, g ^ bit), device_id_type=MESH)

    def side_copy(col, part):
        i = sem(col, 0, part)
        step, slot = (-1, 1) if col == 0 else (1, 0)
        return pltpu.make_async_remote_copy(
            src_ref=acc.at[col, 0, cut(part)], dst_ref=beside.at[slot, cut(part)], send_sem=send_sem.at[i],
            recv_sem=recv_sem.at[i], device_id=(b + step, g), device_id_type=MESH)

    odd = [m for m in masks if m & 1]
    for mask in sorted(odd, reverse=True):
        for part in parts:
            for col in cols:
                under(has[col], lambda: grp_copy(col, mask, part).start())
    for bit in reversed(grp_bits(groups)):
        kept = [m for m in range(groups) if m % (2 * bit) == 0]
        for mask in sorted(kept, reverse=True):
            for part in parts:
                for col in cols:
                    def step():
                        grp_copy(col, mask | bit, part).wait_recv()
                        held = sent.at[col, g ^ mask, cut(part)] if bit == 1 else acc.at[col, mask, cut(part)]
                        add_blocks(acc.at[col, mask, cut(part)], held, land.at[col, mask | bit, cut(part)], span)
                        if mask and low_bit(mask) == 2 * bit:
                            grp_copy(col, mask, part).start()
                        if 2 * bit == groups and col != 1:
                            side_copy(col, part).start()
                    under(has[col], step)
    for part in parts:
        for col in (0, 2):
            pl.when(has[opposite[col]])(lambda: side_copy(col, part).wait_recv())
    for part in parts:
        for col in (0, 2):
            pl.when(has[col])(lambda: side_copy(col, part).wait_send())
        for mask in masks:
            for col in cols:
                under(has[col], lambda: grp_copy(col, mask, part).wait_send())


def reduced_rows(own, acc, beside, total, columns):
    _, _, has = where_am_i(columns)
    for i in range(total.shape[0]):
        total[i] = own[i] + acc[1, 0, i].astype(F32)
    for slot, col in ((0, 0), (1, 2)):
        @pl.when(has[col])
        def _():
            for i in range(total.shape[0]):
                total[i] += beside[slot, i].astype(F32)


def rows_below(count, shape):
    return lax.broadcasted_iota(jnp.int32, shape, 0) < count


def spread_features(columns, counts, features, near, send_sem, recv_sem):
    _, g, _ = where_am_i(columns)
    blocks = features.shape[0]
    for i in range(blocks):
        rows = features[i].astype(F32)
        near[1, g, i] = jnp.where(rows_below(counts[i], rows.shape), rows, 0.0).astype(BF16)
    greet(columns, near.shape[1])
    spread(near, send_sem, recv_sem, columns)


def finish_forward(columns, counts, own, sent, cotangent, activated, near,
                   acc, land, beside, total, send_sem, recv_sem, send_sem2, recv_sem2):
    _, g, _ = where_am_i(columns)
    greet(columns, near.shape[1])
    gather_back(sent, acc, land, beside, send_sem, recv_sem, columns)
    reduced_rows(own, acc, beside, total, columns)
    for i in range(total.shape[0]):
        keep = rows_below(counts[i], total.shape[1:])
        pre = jnp.where(keep, total[i], 0.0)
        sig = jax.nn.sigmoid(pre)
        activated[i] = (pre * sig).astype(BF16)
        slope = sig * (1.0 + pre * (1.0 - sig))
        near[1, g, i] = jnp.where(keep, cotangent[i].astype(F32) * slope, 0.0).astype(BF16)
    spread(near, send_sem2, recv_sem2, columns)


def finish_backward(columns, counts, own, sent, grad, acc, land, beside, total, send_sem, recv_sem):
    greet(columns, sent.shape[1])
    gather_back(sent, acc, land, beside, send_sem, recv_sem, columns)
    reduced_rows(own, acc, beside, total, columns)
    for i in range(total.shape[0]):
        keep = rows_below(counts[i], total.shape[1:])
        grad[i] = jnp.where(keep, total[i], 0.0).astype(BF16)


def dot(a, b):
    return jnp.dot(a, b, preferred_element_type=F32)


def zero_blocks(ref):
    def clear(i, carry):
        ref[i] = jnp.zeros(ref.shape[1:], ref.dtype)
        return carry
    lax.fori_loop(0, ref.shape[0], clear, 0)


def forward_slots(first_of, near_of, base, used, tile, near, weights, mirror_t, own, sent, left, right):
    slot = pl.program_id(0)
    kernels, width = tile.shape[1], near.shape[2]

    @pl.when(slot == 0)
    def _():
        zero_blocks(own)
        zero_blocks(sent)

    @pl.when(slot < used[0])
    def _():
        first, second = first_of[slot], near_of[slot]
        right[...] = dot(near[second], weights[...]).astype(BF16)
        rows_t = near[base[0] + first].astype(F32).T.astype(BF16)
        left[...] = dot(mirror_t[...], rows_t).astype(BF16)
        to_first = jnp.zeros(own.shape[1:], F32)
        to_second = jnp.zeros(own.shape[1:][::-1], F32)
        for k in range(kernels):
            cut = pl.ds(k * width, width)
            to_first += dot(tile[0, k], right[:, cut])
            to_second += dot(left[cut, :], tile[0, k])
        own[first] += to_first
        sent[second] = (sent[second].astype(F32) + to_second.T).astype(BF16)


def backward_slots(first_of, near_of, base, used, tile, near, near_up, weights, mirror_t,
                   own, sent, grad_near, grad_own, up_t, up_own):
    slot = pl.program_id(0)
    kernels, width = tile.shape[1], near.shape[2]

    @pl.when(slot == 0)
    def _():
        zero_blocks(own)
        zero_blocks(sent)
        grad_near[...] = jnp.zeros_like(grad_near)
        grad_own[...] = jnp.zeros_like(grad_own)

    @pl.when(slot < used[0])
    def _():
        first, second = first_of[slot], near_of[slot]
        up_first_t = near_up[base[0] + first].astype(F32).T.astype(BF16)
        up_second = near_up[second]
        for k in range(kernels):
            cut = pl.ds(k * width, width)
            up_t[cut, :] = dot(up_first_t, tile[0, k]).astype(BF16)
            up_own[:, cut] = dot(tile[0, k], up_second).astype(BF16)
        rows_t = near[base[0] + first].astype(F32).T.astype(BF16)
        grad_near[...] += dot(up_t[...], near[second])
        grad_own[...] += dot(rows_t, up_own[...])
        to_second = dot(weights[...], up_t[...])
        own[first] += dot(up_own[...], mirror_t[...])
        sent[second] = (sent[second].astype(F32) + to_second.T).astype(BF16)


def body(features, point_counts, kernel_weights, influence, pair_list, pair_counts, cotangent):
    blocks, points, width = features.shape
    kernels = kernel_weights.shape[0]
    slots = influence.shape[0]
    columns, groups = lax.axis_size("block"), lax.axis_size("grp")
    b, g = lax.axis_index("block"), lax.axis_index("grp")
    region = groups * blocks
    flat = (3 * region, points, width)
    spread_shape = (3, groups, blocks, points, width)
    own_shape = (blocks, points, width)
    copies = 3 * groups * PARTS

    used = pair_counts
    first_of = pair_list[:, 0]
    near_of = pair_list[:, 1] - (b - 1) * region
    base = (region + g * blocks).astype(jnp.int32)[None]
    weights = kernel_weights.transpose(1, 0, 2).reshape(width, kernels * width)
    mirror_t = kernel_weights[::-1].transpose(0, 2, 1).reshape(kernels * width, width)

    def remote(kernel, collective, ins, outs, scratch, args):
        return pl.pallas_call(
            functools.partial(kernel, columns),
            in_specs=ins,
            out_specs=[VMEM] * len(outs),
            out_shape=outs,
            scratch_shapes=scratch,
            compiler_params=pltpu.CompilerParams(
                collective_id=collective, has_side_effects=True, vmem_limit_bytes=VMEM_BYTES),
        )(*args)

    dma = pltpu.SemaphoreType.DMA((copies,))
    reduce_scratch = [
        pltpu.VMEM(spread_shape, BF16), pltpu.VMEM(spread_shape, BF16),
        pltpu.VMEM((2, *own_shape), BF16), pltpu.VMEM(own_shape, F32), dma, dma]
    near_type = jax.ShapeDtypeStruct(spread_shape, BF16)
    own_type = jax.ShapeDtypeStruct(own_shape, BF16)

    def tile_at(slot, first_of, near_of, base, used):
        return (jnp.minimum(slot, used[0] - 1), 0, 0, 0)

    def fixed(shape):
        return pl.BlockSpec(shape, lambda slot, *_: (0,) * len(shape))

    def local(kernel, ins, outs, scratch, args):
        return pl.pallas_call(
            kernel,
            grid_spec=pltpu.PrefetchScalarGridSpec(
                num_scalar_prefetch=4, grid=(slots,),
                in_specs=[pl.BlockSpec((1, kernels, points, points), tile_at)] + [fixed(a.shape) for a in ins],
                out_specs=[fixed(a.shape) for a in outs],
                scratch_shapes=scratch),
            out_shape=outs,
            compiler_params=pltpu.CompilerParams(vmem_limit_bytes=VMEM_BYTES),
        )(first_of, near_of, base, used, influence, *args)

    (near,) = remote(spread_features, 0, [SMEM, VMEM], [near_type], [dma, dma], (point_counts, features))
    near_rows = near.reshape(flat)
    slot_outs = [jax.ShapeDtypeStruct(own_shape, F32), jax.ShapeDtypeStruct(flat, BF16)]
    ins = (near_rows, weights, mirror_t)
    own, sent = local(
        forward_slots, ins, slot_outs,
        [pltpu.VMEM((kernels * width, points), BF16), pltpu.VMEM((points, kernels * width), BF16)], ins)
    activated, near_up = remote(
        finish_forward, 1, [SMEM, VMEM, VMEM, VMEM], [own_type, near_type],
        reduce_scratch + [dma, dma],
        (point_counts, own, sent.reshape(spread_shape), cotangent))
    ins = (near_rows, near_up.reshape(flat), weights, mirror_t)
    own, sent, grad_near, grad_own = local(
        backward_slots, ins,
        slot_outs + [jax.ShapeDtypeStruct((kernels * width, width), F32),
                     jax.ShapeDtypeStruct((width, kernels * width), F32)],
        [pltpu.VMEM((kernels * width, points), BF16), pltpu.VMEM((points, kernels * width), BF16)], ins)
    local_weights = (
        grad_near.reshape(kernels, width, width).transpose(0, 2, 1)
        + grad_own.reshape(width, kernels, width).transpose(1, 0, 2)[::-1])
    total_weights = lax.psum(local_weights, ("block", "grp"))
    (grad_features,) = remote(
        finish_backward, 2, [SMEM, VMEM, VMEM], [own_type], reduce_scratch,
        (point_counts, own, sent.reshape(spread_shape)))
    total_points = blocks * points * columns * groups
    grad_weights = total_weights * (1.0 / math.sqrt(total_points))
    return (activated, grad_features, grad_weights)


def solution(mesh):
    placed = (
        P(("block", "grp"), None, None),
        P(("block", "grp")),
        P(),
        P(("block", "grp"), None, None, None),
        P(("block", "grp"), None),
        P(("block", "grp")),
        P(("block", "grp"), None, None),
    )
    return jax.shard_map(
        body,
        mesh=mesh,
        in_specs=placed,
        out_specs=(P(("block", "grp"), None, None), P(("block", "grp"), None, None), P()),
        check_vma=False,
    )
```

```python
import functools
import math

import jax
import jax.numpy as jnp
from jax import lax
from jax.experimental import pallas as pl
from jax.experimental.pallas import tpu as pltpu
from jax.sharding import PartitionSpec as P

MESH = pl.DeviceIdType.MESH
F32, BF16 = jnp.float32, jnp.bfloat16
VMEM_BYTES = 56 * 2**20
PARTS = 4
VMEM = pl.BlockSpec(memory_space=pltpu.VMEM)
SMEM = pl.BlockSpec(memory_space=pltpu.SMEM)


def low_bit(mask):
    return mask & -mask


def grp_masks(groups):
    return sorted(range(1, groups), key=lambda m: (-low_bit(m), m))


def grp_bits(groups):
    return [1 << i for i in reversed(range(groups.bit_length() - 1))]


def where_am_i(columns):
    b, g = lax.axis_index("block"), lax.axis_index("grp")
    return b, g, {0: b > 0, 1: None, 2: b < columns - 1}


def under(condition, action):
    if condition is None:
        action()
    else:
        pl.when(condition)(action)


def greet(columns, groups, whole_axis=False):
    b, g, has = where_am_i(columns)
    barrier = pltpu.get_barrier_semaphore()
    peers = len(grp_bits(groups))
    for bit in grp_bits(groups):
        pl.semaphore_signal(barrier, inc=1, device_id=(b, g ^ bit), device_id_type=MESH)
    if whole_axis:
        for distance in range(1, columns):
            pl.semaphore_signal(
                barrier, inc=1, device_id=(lax.rem(b + distance, columns), g), device_id_type=MESH)
        peers = peers + columns - 1
    else:
        for side, step in ((0, -1), (2, 1)):
            @pl.when(has[side])
            def _():
                pl.semaphore_signal(barrier, inc=1, device_id=(b + step, g), device_id_type=MESH)
        peers = peers + has[0].astype(jnp.int32) + has[2].astype(jnp.int32)
    pl.semaphore_wait(barrier, peers)


def spread(near, send_sem, recv_sem, columns):
    b, g, has = where_am_i(columns)
    groups, blocks = near.shape[1], near.shape[2]
    span = blocks // PARTS
    opposite = {0: 2, 2: 0}

    def at(col, mask, part):
        return near.at[col, g ^ mask, pl.ds(part * span, span)]

    def sem(col, mask, part):
        return (col * groups + mask) * PARTS + part

    def side_copy(col, part):
        i = sem(col, 0, part)
        step = 1 if col == 0 else -1
        return pltpu.make_async_remote_copy(
            src_ref=at(1, 0, part), dst_ref=at(col, 0, part), send_sem=send_sem.at[i],
            recv_sem=recv_sem.at[i], device_id=(b + step, g), device_id_type=MESH)

    def grp_copy(col, mask, part):
        bit = low_bit(mask)
        i = sem(col, mask, part)
        return pltpu.make_async_remote_copy(
            src_ref=at(col, mask ^ bit, part), dst_ref=at(col, mask ^ bit, part), send_sem=send_sem.at[i],
            recv_sem=recv_sem.at[i], device_id=(b, g ^ bit), device_id_type=MESH)

    def arrival(col, mask, part):
        bit = low_bit(mask)
        i = sem(col, mask, part)
        return pltpu.make_async_remote_copy(
            src_ref=at(col, mask ^ bit, part), dst_ref=at(col, mask, part), send_sem=send_sem.at[i],
            recv_sem=recv_sem.at[i], device_id=(b, g ^ bit), device_id_type=MESH)

    def forward(col, mask, part):
        for bit in grp_bits(groups):
            if mask == 0 or bit < low_bit(mask):
                grp_copy(col, mask | bit, part).start()

    parts = range(PARTS)
    for part in parts:
        for col in (0, 2):
            pl.when(has[opposite[col]])(lambda: side_copy(col, part).start())
        forward(1, 0, part)
    for part in parts:
        for col in (0, 2):
            @pl.when(has[col])
            def _():
                side_copy(col, part).wait_recv()
                forward(col, 0, part)
    masks = grp_masks(groups)
    for mask in masks:
        for part in parts:
            for col in (1, 0, 2):
                def step():
                    arrival(col, mask, part).wait_recv()
                    forward(col, mask, part)
                under(has[col], step)
    for part in parts:
        for col in (0, 2):
            pl.when(has[opposite[col]])(lambda: side_copy(col, part).wait_send())
    for mask in masks:
        for part in parts:
            for col in (0, 1, 2):
                under(has[col], lambda: grp_copy(col, mask, part).wait_send())


def run(*steps):
    for _ in zip(*steps):
        pass
    for step in steps:
        for _ in step:
            pass


def add_blocks(out, one, two, span):
    for i in range(span):
        out[i] = (one[i].astype(F32) + two[i].astype(F32)).astype(BF16)


def gather_back(sent, acc, land, beside, send_sem, recv_sem, columns):
    b, g, has = where_am_i(columns)
    groups, blocks = sent.shape[1], sent.shape[2]
    span = blocks // PARTS
    opposite = {0: 2, 2: 0}
    cols = (0, 2, 1)
    parts = range(PARTS)
    masks = grp_masks(groups)

    def cut(part):
        return pl.ds(part * span, span)

    def sem(col, mask, part):
        return (col * groups + mask) * PARTS + part

    def grp_copy(col, mask, part):
        bit = low_bit(mask)
        i = sem(col, mask, part)
        src = sent.at[col, g ^ mask, cut(part)] if bit == 1 else acc.at[col, mask, cut(part)]
        return pltpu.make_async_remote_copy(
            src_ref=src, dst_ref=land.at[col, mask, cut(part)], send_sem=send_sem.at[i],
            recv_sem=recv_sem.at[i], device_id=(b, g ^ bit), device_id_type=MESH)

    def side_copy(col, part):
        i = sem(col, 0, part)
        step, slot = (-1, 1) if col == 0 else (1, 0)
        return pltpu.make_async_remote_copy(
            src_ref=acc.at[col, 0, cut(part)], dst_ref=beside.at[slot, cut(part)], send_sem=send_sem.at[i],
            recv_sem=recv_sem.at[i], device_id=(b + step, g), device_id_type=MESH)

    odd = [m for m in masks if m & 1]
    for mask in sorted(odd, reverse=True):
        for part in parts:
            for col in cols:
                under(has[col], lambda: grp_copy(col, mask, part).start())
    yield
    for bit in reversed(grp_bits(groups)):
        kept = [m for m in range(groups) if m % (2 * bit) == 0]
        for mask in sorted(kept, reverse=True):
            for part in parts:
                for col in cols:
                    def step():
                        grp_copy(col, mask | bit, part).wait_recv()
                        held = sent.at[col, g ^ mask, cut(part)] if bit == 1 else acc.at[col, mask, cut(part)]
                        add_blocks(acc.at[col, mask, cut(part)], held, land.at[col, mask | bit, cut(part)], span)
                        if mask and low_bit(mask) == 2 * bit:
                            grp_copy(col, mask, part).start()
                        if 2 * bit == groups and col != 1:
                            side_copy(col, part).start()
                    under(has[col], step)
                if 2 * bit == groups and part == PARTS // 2 - 1:
                    yield
            yield
    for part in parts:
        for col in (0, 2):
            pl.when(has[opposite[col]])(lambda: side_copy(col, part).wait_recv())
    for part in parts:
        for col in (0, 2):
            pl.when(has[col])(lambda: side_copy(col, part).wait_send())
        for mask in masks:
            for col in cols:
                under(has[col], lambda: grp_copy(col, mask, part).wait_send())


def reduced_rows(own, acc, beside, total, columns):
    _, _, has = where_am_i(columns)
    for i in range(total.shape[0]):
        total[i] = own[i] + acc[1, 0, i].astype(F32)
    for slot, col in ((0, 0), (1, 2)):
        @pl.when(has[col])
        def _():
            for i in range(total.shape[0]):
                total[i] += beside[slot, i].astype(F32)


def rows_below(count, shape):
    return lax.broadcasted_iota(jnp.int32, shape, 0) < count


def spread_features(columns, counts, features, near, send_sem, recv_sem):
    _, g, _ = where_am_i(columns)
    blocks = features.shape[0]
    for i in range(blocks):
        rows = features[i].astype(F32)
        near[1, g, i] = jnp.where(rows_below(counts[i], rows.shape), rows, 0.0).astype(BF16)
    greet(columns, near.shape[1])
    spread(near, send_sem, recv_sem, columns)


def finish_forward(columns, counts, own, sent, cotangent, activated, near,
                   acc, land, beside, total, send_sem, recv_sem, send_sem2, recv_sem2):
    _, g, _ = where_am_i(columns)
    greet(columns, near.shape[1])
    run(gather_back(sent, acc, land, beside, send_sem, recv_sem, columns))
    reduced_rows(own, acc, beside, total, columns)
    for i in range(total.shape[0]):
        keep = rows_below(counts[i], total.shape[1:])
        pre = jnp.where(keep, total[i], 0.0)
        sig = jax.nn.sigmoid(pre)
        activated[i] = (pre * sig).astype(BF16)
        slope = sig * (1.0 + pre * (1.0 - sig))
        near[1, g, i] = jnp.where(keep, cotangent[i].astype(F32) * slope, 0.0).astype(BF16)
    spread(near, send_sem2, recv_sem2, columns)


def sum_weights(scale, terms, out, land, held, low, low_land, mixed, gathered, send_sem, recv_sem, columns):
    b, g, _ = where_am_i(columns)
    groups = terms.shape[0]
    bits = grp_bits(groups)
    base_a, base_b, base_c = groups, groups + columns, groups + 2 * columns
    distances = range(1, columns)

    def copy(src, dst, i, device):
        return pltpu.make_async_remote_copy(
            src_ref=src, dst_ref=dst, send_sem=send_sem.at[i], recv_sem=recv_sem.at[i],
            device_id=device, device_id_type=MESH)

    def halve(mask):
        bit = low_bit(mask)
        if bit == 1:
            return copy(terms.at[g ^ mask], land.at[mask], mask, (b, g ^ bit))
        return copy(low.at[mask], low_land.at[mask], mask, (b, g ^ bit))

    def share(distance):
        peer = lax.rem(b + distance, columns)
        return copy(low.at[0, peer], mixed.at[distance], base_a + distance, (peer, g))

    def tell(distance):
        peer = lax.rem(b + distance, columns)
        return copy(gathered.at[g, b], gathered.at[g, b], base_b + distance, (peer, g))

    def told(distance):
        peer = lax.rem(b + columns - distance, columns)
        return copy(gathered.at[g, b], gathered.at[g, peer], base_b + distance, (peer, g))

    def double(mask):
        piece = gathered.at[g ^ mask ^ low_bit(mask)]
        return copy(piece, piece, base_c + mask, (b, g ^ low_bit(mask)))

    def doubled(mask):
        return copy(gathered.at[g], gathered.at[g ^ mask], base_c + mask, (b, g ^ low_bit(mask)))

    masks = grp_masks(groups)
    for mask in masks:
        if mask & 1:
            halve(mask).start()
    yield
    for bit in reversed(bits):
        for mask in sorted((m for m in range(groups) if m % (2 * bit) == 0), reverse=True):
            halve(mask | bit).wait_recv()
            for n in range(columns):
                if bit == 1:
                    value = terms[g ^ mask, n] + land[mask | 1, n]
                else:
                    value = held[mask, n] + low_land[mask | bit, n].astype(F32)
                held[mask, n] = value
                low[mask, n] = value.astype(BF16)
            if mask and low_bit(mask) == 2 * bit:
                halve(mask).start()
        if 2 * bit == groups:
            for distance in distances:
                share(distance).start()
        yield
    for distance in distances:
        share(distance).wait_recv()
    total = held[0, b]
    for distance in distances:
        total += mixed[distance].astype(F32)
    gathered[g, b] = total.astype(BF16)
    for distance in distances:
        tell(distance).start()
    yield
    for distance in distances:
        told(distance).wait_recv()
    for bit in bits:
        double(bit).start()
    yield
    for mask in masks:
        doubled(mask).wait_recv()
        for bit in bits:
            if bit < low_bit(mask):
                double(mask | bit).start()
        if low_bit(mask) == 2:
            yield
    for mask in masks:
        halve(mask).wait_send()
        double(mask).wait_send()
    for distance in distances:
        share(distance).wait_send()
        tell(distance).wait_send()
    for h in range(groups):
        out[h] = gathered[h].astype(F32) * scale


def finish_backward(scale, columns, counts, own, sent, terms, grad, summed, acc, land, beside, total, send_sem, recv_sem,
                    w_land, w_held, w_low, w_low_land, w_mixed, w_gathered, w_send, w_recv):
    greet(columns, sent.shape[1], True)
    run(sum_weights(scale, terms, summed, w_land, w_held, w_low, w_low_land, w_mixed, w_gathered, w_send, w_recv, columns),
        gather_back(sent, acc, land, beside, send_sem, recv_sem, columns))
    reduced_rows(own, acc, beside, total, columns)
    for i in range(total.shape[0]):
        keep = rows_below(counts[i], total.shape[1:])
        grad[i] = jnp.where(keep, total[i], 0.0).astype(BF16)


def dot(a, b):
    return jnp.dot(a, b, preferred_element_type=F32)


def zero_blocks(ref):
    def clear(i, carry):
        ref[i] = jnp.zeros(ref.shape[1:], ref.dtype)
        return carry
    lax.fori_loop(0, ref.shape[0], clear, 0)


def forward_slots(first_of, near_of, base, used, tile, near, weights, mirror_t, own, sent, left, right):
    slot = pl.program_id(0)
    kernels, width = tile.shape[1], near.shape[2]

    @pl.when(slot == 0)
    def _():
        zero_blocks(own)
        zero_blocks(sent)

    @pl.when(slot < used[0])
    def _():
        first, second = first_of[slot], near_of[slot]
        right[...] = dot(near[second], weights[...]).astype(BF16)
        rows_t = near[base[0] + first].astype(F32).T.astype(BF16)
        left[...] = dot(mirror_t[...], rows_t).astype(BF16)
        to_first = jnp.zeros(own.shape[1:], F32)
        to_second = jnp.zeros(own.shape[1:][::-1], F32)
        for k in range(kernels):
            cut = pl.ds(k * width, width)
            to_first += dot(tile[0, k], right[:, cut])
            to_second += dot(left[cut, :], tile[0, k])
        own[first] += to_first
        sent[second] = (sent[second].astype(F32) + to_second.T).astype(BF16)


def backward_slots(first_of, near_of, base, used, tile, near, near_up, weights, mirror_t,
                   own, sent, grads, grad_near, grad_own, up_t, up_own):
    slot = pl.program_id(0)
    kernels, width = tile.shape[1], near.shape[2]

    @pl.when(slot == 0)
    def _():
        zero_blocks(own)
        zero_blocks(sent)
        grad_near[...] = jnp.zeros_like(grad_near)
        grad_own[...] = jnp.zeros_like(grad_own)

    @pl.when(slot < used[0])
    def _():
        first, second = first_of[slot], near_of[slot]
        up_first_t = near_up[base[0] + first].astype(F32).T.astype(BF16)
        up_second = near_up[second]
        for k in range(kernels):
            cut = pl.ds(k * width, width)
            up_t[cut, :] = dot(up_first_t, tile[0, k]).astype(BF16)
            up_own[:, cut] = dot(tile[0, k], up_second).astype(BF16)
        rows_t = near[base[0] + first].astype(F32).T.astype(BF16)
        grad_near[...] += dot(up_t[...], near[second])
        grad_own[...] += dot(rows_t, up_own[...])
        to_second = dot(weights[...], up_t[...])
        own[first] += dot(up_own[...], mirror_t[...])
        sent[second] = (sent[second].astype(F32) + to_second.T).astype(BF16)

    @pl.when(slot == pl.num_programs(0) - 1)
    def _():
        for k in range(kernels):
            mirrored = kernels - 1 - k
            grads[k] = grad_near[k * width:(k + 1) * width, :].T + grad_own[:, mirrored * width:(mirrored + 1) * width]
        for k in range(kernels, grads.shape[0]):
            grads[k] = jnp.zeros(grads.shape[1:], F32)


def body(features, point_counts, kernel_weights, influence, pair_list, pair_counts, cotangent):
    blocks, points, width = features.shape
    kernels = kernel_weights.shape[0]
    slots = influence.shape[0]
    columns, groups = lax.axis_size("block"), lax.axis_size("grp")
    b, g = lax.axis_index("block"), lax.axis_index("grp")
    region = groups * blocks
    flat = (3 * region, points, width)
    spread_shape = (3, groups, blocks, points, width)
    own_shape = (blocks, points, width)
    copies = 3 * groups * PARTS

    used = pair_counts
    first_of = pair_list[:, 0]
    near_of = pair_list[:, 1] - (b - 1) * region
    base = (region + g * blocks).astype(jnp.int32)[None]
    weights = kernel_weights.transpose(1, 0, 2).reshape(width, kernels * width)
    mirror_t = kernel_weights[::-1].transpose(0, 2, 1).reshape(kernels * width, width)

    def remote(kernel, collective, ins, outs, scratch, args):
        return pl.pallas_call(
            functools.partial(kernel, columns),
            in_specs=ins,
            out_specs=[VMEM] * len(outs),
            out_shape=outs,
            scratch_shapes=scratch,
            compiler_params=pltpu.CompilerParams(
                collective_id=collective, has_side_effects=True, vmem_limit_bytes=VMEM_BYTES),
        )(*args)

    dma = pltpu.SemaphoreType.DMA((copies,))
    reduce_scratch = [
        pltpu.VMEM(spread_shape, BF16), pltpu.VMEM(spread_shape, BF16),
        pltpu.VMEM((2, *own_shape), BF16), pltpu.VMEM(own_shape, F32), dma, dma]
    near_type = jax.ShapeDtypeStruct(spread_shape, BF16)
    own_type = jax.ShapeDtypeStruct(own_shape, BF16)

    def tile_at(slot, first_of, near_of, base, used):
        return (jnp.minimum(slot, used[0] - 1), 0, 0, 0)

    def fixed(shape):
        return pl.BlockSpec(shape, lambda slot, *_: (0,) * len(shape))

    def local(kernel, ins, outs, scratch, args):
        return pl.pallas_call(
            kernel,
            grid_spec=pltpu.PrefetchScalarGridSpec(
                num_scalar_prefetch=4, grid=(slots,),
                in_specs=[pl.BlockSpec((1, kernels, points, points), tile_at)] + [fixed(a.shape) for a in ins],
                out_specs=[fixed(a.shape) for a in outs],
                scratch_shapes=scratch),
            out_shape=outs,
            compiler_params=pltpu.CompilerParams(vmem_limit_bytes=VMEM_BYTES),
        )(first_of, near_of, base, used, influence, *args)

    (near,) = remote(spread_features, 0, [SMEM, VMEM], [near_type], [dma, dma], (point_counts, features))
    near_rows = near.reshape(flat)
    slot_outs = [jax.ShapeDtypeStruct(own_shape, F32), jax.ShapeDtypeStruct(flat, BF16)]
    ins = (near_rows, weights, mirror_t)
    own, sent = local(
        forward_slots, ins, slot_outs,
        [pltpu.VMEM((kernels * width, points), BF16), pltpu.VMEM((points, kernels * width), BF16)], ins)
    activated, near_up = remote(
        finish_forward, 1, [SMEM, VMEM, VMEM, VMEM], [own_type, near_type],
        reduce_scratch + [dma, dma],
        (point_counts, own, sent.reshape(spread_shape), cotangent))
    ins = (near_rows, near_up.reshape(flat), weights, mirror_t)
    share = 16 * columns * groups
    padded = -(-kernels * width // share) * share // width
    own, sent, grads = local(
        backward_slots, ins, slot_outs + [jax.ShapeDtypeStruct((padded, width, width), F32)],
        [pltpu.VMEM((kernels * width, width), F32), pltpu.VMEM((width, kernels * width), F32),
         pltpu.VMEM((kernels * width, points), BF16), pltpu.VMEM((points, kernels * width), BF16)], ins)
    scale = 1.0 / math.sqrt(blocks * points * columns * groups)
    cut = (groups, columns, padded * width // (groups * columns), width)
    w_dma = pltpu.SemaphoreType.DMA((2 * groups + 2 * columns,))
    grad_features, summed = remote(
        functools.partial(finish_backward, scale), 2, [SMEM, VMEM, VMEM, VMEM],
        [own_type, jax.ShapeDtypeStruct(cut, F32)],
        reduce_scratch + [
            pltpu.VMEM(cut, F32), pltpu.VMEM(cut, F32), pltpu.VMEM(cut, BF16), pltpu.VMEM(cut, BF16),
            pltpu.VMEM(cut[1:], BF16), pltpu.VMEM(cut, BF16), w_dma, w_dma],
        (point_counts, own, sent.reshape(spread_shape), grads.reshape(cut)))
    grad_weights = summed.reshape(padded, width, width)[:kernels]
    return (activated, grad_features, grad_weights)


def solution(mesh):
    placed = (
        P(("block", "grp"), None, None),
        P(("block", "grp")),
        P(),
        P(("block", "grp"), None, None, None),
        P(("block", "grp"), None),
        P(("block", "grp")),
        P(("block", "grp"), None, None),
    )
    return jax.shard_map(
        body,
        mesh=mesh,
        in_specs=placed,
        out_specs=(P(("block", "grp"), None, None), P(("block", "grp"), None, None), P()),
        check_vma=False,
    )
```

```python
import functools
import math

import jax
import jax.numpy as jnp
from jax import lax
from jax.experimental import pallas as pl
from jax.experimental.pallas import tpu as pltpu
from jax.sharding import PartitionSpec as P

MESH = pl.DeviceIdType.MESH
F32, BF16 = jnp.float32, jnp.bfloat16
VMEM_BYTES = 56 * 2**20
PARTS = 4
VMEM = pl.BlockSpec(memory_space=pltpu.VMEM)
SMEM = pl.BlockSpec(memory_space=pltpu.SMEM)


def low_bit(mask):
    return mask & -mask


def grp_masks(groups):
    return sorted(range(1, groups), key=lambda m: (-low_bit(m), m))


def grp_bits(groups):
    return [1 << i for i in reversed(range(groups.bit_length() - 1))]


def where_am_i(columns):
    b, g = lax.axis_index("block"), lax.axis_index("grp")
    return b, g, {0: b > 0, 1: None, 2: b < columns - 1}


def under(condition, action):
    if condition is None:
        action()
    else:
        pl.when(condition)(action)


def greet(columns, groups, whole_axis=False):
    b, g, has = where_am_i(columns)
    barrier = pltpu.get_barrier_semaphore()
    peers = len(grp_bits(groups))
    for bit in grp_bits(groups):
        pl.semaphore_signal(barrier, inc=1, device_id=(b, g ^ bit), device_id_type=MESH)
    if whole_axis:
        for distance in range(1, columns):
            pl.semaphore_signal(
                barrier, inc=1, device_id=(lax.rem(b + distance, columns), g), device_id_type=MESH)
        peers = peers + columns - 1
    else:
        for side, step in ((0, -1), (2, 1)):
            @pl.when(has[side])
            def _():
                pl.semaphore_signal(barrier, inc=1, device_id=(b + step, g), device_id_type=MESH)
        peers = peers + has[0].astype(jnp.int32) + has[2].astype(jnp.int32)
    pl.semaphore_wait(barrier, peers)


def spread(near, send_sem, recv_sem, columns):
    b, g, has = where_am_i(columns)
    groups, blocks = near.shape[1], near.shape[2]
    span = blocks // PARTS
    opposite = {0: 2, 2: 0}

    def at(col, mask, part):
        return near.at[col, g ^ mask, pl.ds(part * span, span)]

    def sem(col, mask, part):
        return (col * groups + mask) * PARTS + part

    def side_copy(col, part):
        i = sem(col, 0, part)
        step = 1 if col == 0 else -1
        return pltpu.make_async_remote_copy(
            src_ref=at(1, 0, part), dst_ref=at(col, 0, part), send_sem=send_sem.at[i],
            recv_sem=recv_sem.at[i], device_id=(b + step, g), device_id_type=MESH)

    def grp_copy(col, mask, part):
        bit = low_bit(mask)
        i = sem(col, mask, part)
        return pltpu.make_async_remote_copy(
            src_ref=at(col, mask ^ bit, part), dst_ref=at(col, mask ^ bit, part), send_sem=send_sem.at[i],
            recv_sem=recv_sem.at[i], device_id=(b, g ^ bit), device_id_type=MESH)

    def arrival(col, mask, part):
        bit = low_bit(mask)
        i = sem(col, mask, part)
        return pltpu.make_async_remote_copy(
            src_ref=at(col, mask ^ bit, part), dst_ref=at(col, mask, part), send_sem=send_sem.at[i],
            recv_sem=recv_sem.at[i], device_id=(b, g ^ bit), device_id_type=MESH)

    def forward(col, mask, part):
        for bit in grp_bits(groups):
            if mask == 0 or bit < low_bit(mask):
                grp_copy(col, mask | bit, part).start()

    parts = range(PARTS)
    for part in parts:
        for col in (0, 2):
            pl.when(has[opposite[col]])(lambda: side_copy(col, part).start())
        forward(1, 0, part)
    yield
    for part in parts:
        for col in (0, 2):
            @pl.when(has[col])
            def _():
                side_copy(col, part).wait_recv()
                forward(col, 0, part)
    yield
    masks = grp_masks(groups)
    for mask in masks:
        for part in parts:
            for col in (1, 0, 2):
                def step():
                    arrival(col, mask, part).wait_recv()
                    forward(col, mask, part)
                under(has[col], step)
    for part in parts:
        for col in (0, 2):
            pl.when(has[opposite[col]])(lambda: side_copy(col, part).wait_send())
    for mask in masks:
        for part in parts:
            for col in (0, 1, 2):
                under(has[col], lambda: grp_copy(col, mask, part).wait_send())


def run(*steps):
    for _ in zip(*steps):
        pass
    for step in steps:
        for _ in step:
            pass


def add_blocks(out, one, two, span):
    for i in range(span):
        out[i] = (one[i].astype(F32) + two[i].astype(F32)).astype(BF16)


def gather_back(sent, acc, land, beside, send_sem, recv_sem, columns):
    b, g, has = where_am_i(columns)
    groups, blocks = sent.shape[1], sent.shape[2]
    span = blocks // PARTS
    opposite = {0: 2, 2: 0}
    cols = (0, 2, 1)
    parts = range(PARTS)
    masks = grp_masks(groups)

    def cut(part):
        return pl.ds(part * span, span)

    def sem(col, mask, part):
        return (col * groups + mask) * PARTS + part

    def grp_copy(col, mask, part):
        bit = low_bit(mask)
        i = sem(col, mask, part)
        src = sent.at[col, g ^ mask, cut(part)] if bit == 1 else acc.at[col, mask, cut(part)]
        return pltpu.make_async_remote_copy(
            src_ref=src, dst_ref=land.at[col, mask, cut(part)], send_sem=send_sem.at[i],
            recv_sem=recv_sem.at[i], device_id=(b, g ^ bit), device_id_type=MESH)

    def side_copy(col, part):
        i = sem(col, 0, part)
        step, slot = (-1, 1) if col == 0 else (1, 0)
        return pltpu.make_async_remote_copy(
            src_ref=acc.at[col, 0, cut(part)], dst_ref=beside.at[slot, cut(part)], send_sem=send_sem.at[i],
            recv_sem=recv_sem.at[i], device_id=(b + step, g), device_id_type=MESH)

    odd = [m for m in masks if m & 1]
    for mask in sorted(odd, reverse=True):
        for part in parts:
            for col in cols:
                under(has[col], lambda: grp_copy(col, mask, part).start())
    yield
    for bit in reversed(grp_bits(groups)):
        kept = [m for m in range(groups) if m % (2 * bit) == 0]
        for mask in sorted(kept, reverse=True):
            for part in parts:
                for col in cols:
                    def step():
                        grp_copy(col, mask | bit, part).wait_recv()
                        held = sent.at[col, g ^ mask, cut(part)] if bit == 1 else acc.at[col, mask, cut(part)]
                        add_blocks(acc.at[col, mask, cut(part)], held, land.at[col, mask | bit, cut(part)], span)
                        if mask and low_bit(mask) == 2 * bit:
                            grp_copy(col, mask, part).start()
                        if 2 * bit == groups and col != 1:
                            side_copy(col, part).start()
                    under(has[col], step)
                if 2 * bit == groups and part == PARTS // 2 - 1:
                    yield
            yield
    for part in parts:
        for col in (0, 2):
            pl.when(has[opposite[col]])(lambda: side_copy(col, part).wait_recv())
    for part in parts:
        for col in (0, 2):
            pl.when(has[col])(lambda: side_copy(col, part).wait_send())
        for mask in masks:
            for col in cols:
                under(has[col], lambda: grp_copy(col, mask, part).wait_send())


def dot(a, b):
    return jnp.dot(a, b, preferred_element_type=F32)


def clear_edges(near, columns):
    _, _, has = where_am_i(columns)
    for col in (0, 2):
        @pl.when(jnp.logical_not(has[col]))
        def _():
            def clear(h, carry):
                for x in range(near.shape[2]):
                    near[col, h, x] = jnp.zeros(near.shape[3:], near.dtype)
                return carry
            lax.fori_loop(0, near.shape[1], clear, 0)


class Tables:
    def __init__(self, ref, slots, blocks):
        self.ref, self.slots, self.blocks = ref, slots, blocks

    def entry(self, row, slot):
        return self.ref[row * self.slots + slot]

    def first(self, slot):
        return self.entry(0, slot)

    def second(self, slot):
        return self.entry(1, slot), self.entry(2, slot), self.entry(3, slot)

    def flag(self, slot):
        return self.entry(4, slot).astype(F32)

    def before_first(self, slot):
        return self.entry(5, slot)

    def before_second(self, slot):
        return self.entry(6, slot)

    def last_first(self, block):
        return self.ref[7 * self.slots + block]

    def last_second(self, place):
        return self.ref[7 * self.slots + self.blocks + place]


def table_of(pair_list, used, column, blocks, groups):
    slots = pair_list.shape[0]
    index = jnp.arange(slots, dtype=jnp.int32)
    active = index < used
    first = pair_list[:, 0]
    owner = pair_list[:, 1] // blocks
    col, h, x = owner // groups - column + 1, owner % groups, pair_list[:, 1] % blocks
    place = (col * groups + h) * blocks + x

    def latest(match):
        return jnp.max(jnp.where(match, index[None, :], -1), axis=1)

    def chain(key, keys):
        earlier = (key[:, None] == key[None, :]) & active[None, :] & (index[None, :] < index[:, None])
        found = latest(earlier)
        here = latest((jnp.arange(keys, dtype=jnp.int32)[:, None] == key[None, :]) & active[None, :])
        return jnp.where(found < 0, slots, found), jnp.where(here < 0, slots, here)

    before_first, last_first = chain(first, blocks)
    before_second, last_second = chain(place, 3 * groups * blocks)
    return jnp.concatenate([first, col, h, x, active.astype(jnp.int32), before_first, before_second, last_first, last_second])


def fetch(influence, tiles, tile_sem, slot):
    return pltpu.make_async_copy(influence.at[slot], tiles.at[slot], tile_sem.at[slot])


def fill_sent(sent, tables, message):
    groups, blocks = sent.shape[1], sent.shape[2]
    for col in range(3):
        def place(h, carry):
            for x in range(blocks):
                sent[col, h, x] = message[tables.last_second((col * groups + h) * blocks + x)].astype(BF16)
            return carry
        lax.fori_loop(0, groups, place, 0)


def reduced_rows(tables, message, acc, beside, total, columns):
    _, _, has = where_am_i(columns)
    for i in range(total.shape[0]):
        total[i] = message[tables.last_first(i)] + acc[1, 0, i].astype(F32)
    for slot, col in ((0, 0), (1, 2)):
        @pl.when(has[col])
        def _():
            for i in range(total.shape[0]):
                total[i] += beside[slot, i].astype(F32)


def rows_below(count, shape):
    return lax.broadcasted_iota(jnp.int32, shape, 0) < count


def halves(slots, work):
    middle = slots // 2
    for start, end in ((0, middle), (middle, slots)):
        def step(slot, carry):
            work(slot)
            return carry
        yield lambda: lax.fori_loop(start, end, step, 0)


def forward_pass(columns, counts, table, features, influence, weights, mirror_t, cotangent,
                 activated, upstream, near,
                 mine, tiles, left, right, to_second, to_first, sent,
                 acc, land, beside, total, tile_sem, send_sem, recv_sem, send_sem2, recv_sem2):
    _, g, _ = where_am_i(columns)
    slots, kernels, width = tiles.shape[0], tiles.shape[1], features.shape[2]
    tables = Tables(table, slots, features.shape[0])
    for slot in range(slots):
        fetch(influence, tiles, tile_sem, slot).start()
    for i in range(features.shape[0]):
        rows = features[i].astype(F32)
        rows = jnp.where(rows_below(counts[i], rows.shape), rows, 0.0).astype(BF16)
        mine[i] = rows
        near[1, g, i] = rows
    clear_edges(near, columns)
    to_second[slots] = jnp.zeros(to_second.shape[1:], F32)
    to_first[slots] = jnp.zeros(to_first.shape[1:], F32)

    def own_terms(slot):
        fetch(influence, tiles, tile_sem, slot).wait()
        rows_t = mine[tables.first(slot)].astype(F32).T.astype(BF16)
        left[...] = dot(mirror_t[...], rows_t).astype(BF16)
        value = jnp.zeros(to_second.shape[1:][::-1], F32)
        for k in range(kernels):
            value += dot(left[k * width:(k + 1) * width, :], tiles[slot, k])
        to_second[slot] = value.T + to_second[tables.before_second(slot)]

    def near_terms(slot):
        col, h, x = tables.second(slot)
        right[...] = dot(near[col, h, x], weights[...]).astype(BF16)
        value = jnp.zeros(to_first.shape[1:], F32)
        for k in range(kernels):
            value += dot(tiles[slot, k], right[:, k * width:(k + 1) * width])
        to_first[slot] = value + to_first[tables.before_first(slot)]

    greet(columns, near.shape[1])
    work = halves(slots, own_terms)
    steps = spread(near, send_sem, recv_sem, columns)
    next(steps)
    next(work)()
    next(steps)
    next(work)()
    run(steps)
    fill_sent(sent, tables, to_second)
    work = halves(slots, near_terms)
    steps = gather_back(sent, acc, land, beside, send_sem2, recv_sem2, columns)
    next(steps)
    next(steps)
    next(work)()
    next(steps)
    next(steps)
    next(work)()
    run(steps)
    reduced_rows(tables, to_first, acc, beside, total, columns)
    for i in range(total.shape[0]):
        keep = rows_below(counts[i], total.shape[1:])
        pre = jnp.where(keep, total[i], 0.0)
        sig = jax.nn.sigmoid(pre)
        activated[i] = (pre * sig).astype(BF16)
        slope = sig * (1.0 + pre * (1.0 - sig))
        upstream[i] = jnp.where(keep, cotangent[i].astype(F32) * slope, 0.0).astype(BF16)


def sum_weights(scale, terms, out, land, held, low, low_land, mixed, gathered, send_sem, recv_sem, columns):
    b, g, _ = where_am_i(columns)
    groups = terms.shape[0]
    bits = grp_bits(groups)
    base_a, base_b, base_c = groups, groups + columns, groups + 2 * columns
    distances = range(1, columns)

    def copy(src, dst, i, device):
        return pltpu.make_async_remote_copy(
            src_ref=src, dst_ref=dst, send_sem=send_sem.at[i], recv_sem=recv_sem.at[i],
            device_id=device, device_id_type=MESH)

    def halve(mask):
        bit = low_bit(mask)
        if bit == 1:
            return copy(terms.at[g ^ mask], land.at[mask], mask, (b, g ^ bit))
        return copy(low.at[mask], low_land.at[mask], mask, (b, g ^ bit))

    def share(distance):
        peer = lax.rem(b + distance, columns)
        return copy(low.at[0, peer], mixed.at[distance], base_a + distance, (peer, g))

    def tell(distance):
        peer = lax.rem(b + distance, columns)
        return copy(gathered.at[g, b], gathered.at[g, b], base_b + distance, (peer, g))

    def told(distance):
        peer = lax.rem(b + columns - distance, columns)
        return copy(gathered.at[g, b], gathered.at[g, peer], base_b + distance, (peer, g))

    def double(mask):
        piece = gathered.at[g ^ mask ^ low_bit(mask)]
        return copy(piece, piece, base_c + mask, (b, g ^ low_bit(mask)))

    def doubled(mask):
        return copy(gathered.at[g], gathered.at[g ^ mask], base_c + mask, (b, g ^ low_bit(mask)))

    masks = grp_masks(groups)
    for mask in masks:
        if mask & 1:
            halve(mask).start()
    yield
    for bit in reversed(bits):
        for mask in sorted((m for m in range(groups) if m % (2 * bit) == 0), reverse=True):
            halve(mask | bit).wait_recv()
            for n in range(columns):
                if bit == 1:
                    value = terms[g ^ mask, n] + land[mask | 1, n]
                else:
                    value = held[mask, n] + low_land[mask | bit, n].astype(F32)
                held[mask, n] = value
                low[mask, n] = value.astype(BF16)
            if mask and low_bit(mask) == 2 * bit:
                halve(mask).start()
        if 2 * bit == groups:
            for distance in distances:
                share(distance).start()
        yield
    for distance in distances:
        share(distance).wait_recv()
    total = held[0, b]
    for distance in distances:
        total += mixed[distance].astype(F32)
    gathered[g, b] = total.astype(BF16)
    for distance in distances:
        tell(distance).start()
    yield
    for distance in distances:
        told(distance).wait_recv()
    for bit in bits:
        double(bit).start()
    yield
    for mask in masks:
        doubled(mask).wait_recv()
        for bit in bits:
            if bit < low_bit(mask):
                double(mask | bit).start()
        if low_bit(mask) == 2:
            yield
    for mask in masks:
        halve(mask).wait_send()
        double(mask).wait_send()
    for distance in distances:
        share(distance).wait_send()
        tell(distance).wait_send()
    for h in range(groups):
        out[h] = gathered[h].astype(F32) * scale


def backward_pass(scale, columns, counts, table, near, upstream, influence, weights, mirror_t,
                  grad, summed,
                  near_up, tiles, up_t, up_own, grad_near, grad_own, grads, to_second, to_first, sent,
                  acc, land, beside, total, tile_sem, send_sem, recv_sem, send_sem2, recv_sem2,
                  w_land, w_held, w_low, w_low_land, w_mixed, w_gathered, w_send, w_recv):
    _, g, _ = where_am_i(columns)
    slots, kernels, width = tiles.shape[0], tiles.shape[1], upstream.shape[2]
    tables = Tables(table, slots, upstream.shape[0])
    for slot in range(slots):
        fetch(influence, tiles, tile_sem, slot).start()
    for i in range(upstream.shape[0]):
        near_up[1, g, i] = upstream[i]
    clear_edges(near_up, columns)
    to_second[slots] = jnp.zeros(to_second.shape[1:], F32)
    to_first[slots] = jnp.zeros(to_first.shape[1:], F32)
    grad_near[...] = jnp.zeros_like(grad_near)
    grad_own[...] = jnp.zeros_like(grad_own)

    def near_terms(slot):
        fetch(influence, tiles, tile_sem, slot).wait()
        col, h, x = tables.second(slot)
        up_first_t = (upstream[tables.first(slot)].astype(F32) * tables.flag(slot)).T.astype(BF16)
        for k in range(kernels):
            up_t[k * width:(k + 1) * width, :] = dot(up_first_t, tiles[slot, k]).astype(BF16)
        grad_near[...] += dot(up_t[...], near[col, h, x])
        to_second[slot] = dot(weights[...], up_t[...]).T + to_second[tables.before_second(slot)]

    def own_terms(slot):
        col, h, x = tables.second(slot)
        up_second = (near_up[col, h, x].astype(F32) * tables.flag(slot)).astype(BF16)
        for k in range(kernels):
            up_own[:, k * width:(k + 1) * width] = dot(tiles[slot, k], up_second).astype(BF16)
        rows_t = near[1, g, tables.first(slot)].astype(F32).T.astype(BF16)
        grad_own[...] += dot(rows_t, up_own[...])
        to_first[slot] = dot(up_own[...], mirror_t[...]) + to_first[tables.before_first(slot)]

    greet(columns, near.shape[1], True)
    work = halves(slots, near_terms)
    steps = spread(near_up, send_sem, recv_sem, columns)
    next(steps)
    next(work)()
    next(steps)
    next(work)()
    run(steps)
    fill_sent(sent, tables, to_second)
    work = halves(slots, own_terms)
    steps = gather_back(sent, acc, land, beside, send_sem2, recv_sem2, columns)
    next(steps)
    next(steps)
    next(work)()
    next(steps)
    next(work)()
    rows = grads.shape[2]
    shares = width // rows
    for k in range(kernels):
        mirrored = kernels - 1 - k
        value = grad_near[k * width:(k + 1) * width, :].T + grad_own[:, mirrored * width:(mirrored + 1) * width]
        for i in range(shares):
            at = k * shares + i
            grads[at // columns, at % columns] = value[i * rows:(i + 1) * rows]
    for at in range(kernels * shares, grads.shape[0] * columns):
        grads[at // columns, at % columns] = jnp.zeros(grads.shape[2:], F32)
    run(sum_weights(scale, grads, summed, w_land, w_held, w_low, w_low_land, w_mixed, w_gathered, w_send, w_recv, columns),
        steps)
    reduced_rows(tables, to_first, acc, beside, total, columns)
    for i in range(total.shape[0]):
        keep = rows_below(counts[i], total.shape[1:])
        grad[i] = jnp.where(keep, total[i], 0.0).astype(BF16)


def body(features, point_counts, kernel_weights, influence, pair_list, pair_counts, cotangent):
    blocks, points, width = features.shape
    kernels = kernel_weights.shape[0]
    slots = influence.shape[0]
    columns, groups = lax.axis_size("block"), lax.axis_size("grp")
    spread_shape = (3, groups, blocks, points, width)
    own_shape = (blocks, points, width)
    terms = (kernels * width, points)

    table = table_of(pair_list, pair_counts[0], lax.axis_index("block"), blocks, groups)
    weights = kernel_weights.transpose(1, 0, 2).reshape(width, kernels * width)
    mirror_t = kernel_weights[::-1].transpose(0, 2, 1).reshape(kernels * width, width)

    def remote(kernel, collective, ins, outs, scratch, args):
        return pl.pallas_call(
            kernel,
            in_specs=ins,
            out_specs=[VMEM] * len(outs),
            out_shape=outs,
            scratch_shapes=scratch,
            compiler_params=pltpu.CompilerParams(
                collective_id=collective, has_side_effects=True, vmem_limit_bytes=VMEM_BYTES),
        )(*args)

    hbm = pl.BlockSpec(memory_space=pl.ANY)
    dma = pltpu.SemaphoreType.DMA((3 * groups * PARTS,))
    messages = pltpu.VMEM((slots + 1, points, width), F32)
    tiles = pltpu.VMEM(influence.shape, BF16)
    exchange = [
        messages, messages, pltpu.VMEM(spread_shape, BF16),
        pltpu.VMEM(spread_shape, BF16), pltpu.VMEM(spread_shape, BF16),
        pltpu.VMEM((2, *own_shape), BF16), pltpu.VMEM(own_shape, F32),
        pltpu.SemaphoreType.DMA((slots,)), dma, dma, dma, dma]
    near_type = jax.ShapeDtypeStruct(spread_shape, BF16)
    own_type = jax.ShapeDtypeStruct(own_shape, BF16)

    activated, upstream, near = remote(
        functools.partial(forward_pass, columns), 0,
        [SMEM, SMEM, VMEM, hbm, VMEM, VMEM, VMEM], [own_type, own_type, near_type],
        [pltpu.VMEM(own_shape, BF16), tiles, pltpu.VMEM(terms, BF16), pltpu.VMEM(terms[::-1], BF16)] + exchange,
        (point_counts, table, features, influence, weights, mirror_t, cotangent))

    scale = 1.0 / math.sqrt(blocks * points * columns * groups)
    share = 16 * columns * groups
    padded = -(-kernels * width // share) * share // width
    cut = (groups, columns, padded * width // (groups * columns), width)
    w_dma = pltpu.SemaphoreType.DMA((2 * groups + 2 * columns,))
    grad_features, summed = remote(
        functools.partial(backward_pass, scale, columns), 1,
        [SMEM, SMEM, VMEM, VMEM, hbm, VMEM, VMEM], [own_type, jax.ShapeDtypeStruct(cut, F32)],
        [pltpu.VMEM(spread_shape, BF16), tiles, pltpu.VMEM(terms, BF16), pltpu.VMEM(terms[::-1], BF16),
         pltpu.VMEM((kernels * width, width), F32), pltpu.VMEM((width, kernels * width), F32), pltpu.VMEM(cut, F32)]
        + exchange + [
            pltpu.VMEM(cut, F32), pltpu.VMEM(cut, F32), pltpu.VMEM(cut, BF16), pltpu.VMEM(cut, BF16),
            pltpu.VMEM(cut[1:], BF16), pltpu.VMEM(cut, BF16), w_dma, w_dma],
        (point_counts, table, near, upstream, influence, weights, mirror_t))
    grad_weights = summed.reshape(padded, width, width)[:kernels]
    return (activated, grad_features, grad_weights)


def solution(mesh):
    placed = (
        P(("block", "grp"), None, None),
        P(("block", "grp")),
        P(),
        P(("block", "grp"), None, None, None),
        P(("block", "grp"), None),
        P(("block", "grp")),
        P(("block", "grp"), None, None),
    )
    return jax.shard_map(
        body,
        mesh=mesh,
        in_specs=placed,
        out_specs=(P(("block", "grp"), None, None), P(("block", "grp"), None, None), P()),
        check_vma=False,
    )
```

```python
import functools
import math

import jax
import jax.numpy as jnp
from jax import lax
from jax.experimental import pallas as pl
from jax.experimental.pallas import tpu as pltpu
from jax.sharding import PartitionSpec as P

MESH = pl.DeviceIdType.MESH
F32, BF16 = jnp.float32, jnp.bfloat16
VMEM_BYTES = 56 * 2**20
PARTS = 4
VMEM = pl.BlockSpec(memory_space=pltpu.VMEM)
SMEM = pl.BlockSpec(memory_space=pltpu.SMEM)


def low_bit(mask):
    return mask & -mask


def grp_masks(groups):
    return sorted(range(1, groups), key=lambda m: (-low_bit(m), m))


def grp_bits(groups):
    return [1 << i for i in reversed(range(groups.bit_length() - 1))]


def where_am_i(columns):
    b, g = lax.axis_index("block"), lax.axis_index("grp")
    return b, g, {0: b > 0, 1: None, 2: b < columns - 1}


def under(condition, action):
    if condition is None:
        action()
    else:
        pl.when(condition)(action)


def greet(columns, groups, whole_axis=False):
    b, g, has = where_am_i(columns)
    barrier = pltpu.get_barrier_semaphore()
    peers = len(grp_bits(groups))
    for bit in grp_bits(groups):
        pl.semaphore_signal(barrier, inc=1, device_id=(b, g ^ bit), device_id_type=MESH)
    if whole_axis:
        for distance in range(1, columns):
            pl.semaphore_signal(
                barrier, inc=1, device_id=(lax.rem(b + distance, columns), g), device_id_type=MESH)
        peers = peers + columns - 1
    else:
        for side, step in ((0, -1), (2, 1)):
            @pl.when(has[side])
            def _():
                pl.semaphore_signal(barrier, inc=1, device_id=(b + step, g), device_id_type=MESH)
        peers = peers + has[0].astype(jnp.int32) + has[2].astype(jnp.int32)
    pl.semaphore_wait(barrier, peers)


def spread(near, send_sem, recv_sem, columns):
    b, g, has = where_am_i(columns)
    groups, blocks = near.shape[1], near.shape[2]
    span = blocks // PARTS
    opposite = {0: 2, 2: 0}

    def at(col, mask, part):
        return near.at[col, g ^ mask, pl.ds(part * span, span)]

    def sem(col, mask, part):
        return (col * groups + mask) * PARTS + part

    def side_copy(col, part):
        i = sem(col, 0, part)
        step = 1 if col == 0 else -1
        return pltpu.make_async_remote_copy(
            src_ref=at(1, 0, part), dst_ref=at(col, 0, part), send_sem=send_sem.at[i],
            recv_sem=recv_sem.at[i], device_id=(b + step, g), device_id_type=MESH)

    def grp_copy(col, mask, part):
        bit = low_bit(mask)
        i = sem(col, mask, part)
        return pltpu.make_async_remote_copy(
            src_ref=at(col, mask ^ bit, part), dst_ref=at(col, mask ^ bit, part), send_sem=send_sem.at[i],
            recv_sem=recv_sem.at[i], device_id=(b, g ^ bit), device_id_type=MESH)

    def arrival(col, mask, part):
        bit = low_bit(mask)
        i = sem(col, mask, part)
        return pltpu.make_async_remote_copy(
            src_ref=at(col, mask ^ bit, part), dst_ref=at(col, mask, part), send_sem=send_sem.at[i],
            recv_sem=recv_sem.at[i], device_id=(b, g ^ bit), device_id_type=MESH)

    def forward(col, mask, part):
        for bit in grp_bits(groups):
            if mask == 0 or bit < low_bit(mask):
                grp_copy(col, mask | bit, part).start()

    parts = range(PARTS)
    for part in parts:
        for col in (0, 2):
            pl.when(has[opposite[col]])(lambda: side_copy(col, part).start())
        forward(1, 0, part)
    yield
    for part in parts:
        for col in (0, 2):
            @pl.when(has[col])
            def _():
                side_copy(col, part).wait_recv()
                forward(col, 0, part)
    yield
    masks = grp_masks(groups)
    for mask in masks:
        for part in parts:
            for col in (1, 0, 2):
                def step():
                    arrival(col, mask, part).wait_recv()
                    forward(col, mask, part)
                under(has[col], step)
    for part in parts:
        for col in (0, 2):
            pl.when(has[opposite[col]])(lambda: side_copy(col, part).wait_send())
    for mask in masks:
        for part in parts:
            for col in (0, 1, 2):
                under(has[col], lambda: grp_copy(col, mask, part).wait_send())


def run(*steps):
    for _ in zip(*steps):
        pass
    for step in steps:
        for _ in step:
            pass


def add_blocks(out, one, two, span):
    for i in range(span):
        out[i] = (one[i].astype(F32) + two[i].astype(F32)).astype(BF16)


def gather_back(sent, acc, land, beside, send_sem, recv_sem, columns):
    b, g, has = where_am_i(columns)
    groups, blocks = sent.shape[1], sent.shape[2]
    span = blocks // PARTS
    opposite = {0: 2, 2: 0}
    cols = (0, 2, 1)
    parts = range(PARTS)
    masks = grp_masks(groups)

    def cut(part):
        return pl.ds(part * span, span)

    def sem(col, mask, part):
        return (col * groups + mask) * PARTS + part

    def grp_copy(col, mask, part):
        bit = low_bit(mask)
        i = sem(col, mask, part)
        src = sent.at[col, g ^ mask, cut(part)] if bit == 1 else acc.at[col, mask, cut(part)]
        return pltpu.make_async_remote_copy(
            src_ref=src, dst_ref=land.at[col, mask, cut(part)], send_sem=send_sem.at[i],
            recv_sem=recv_sem.at[i], device_id=(b, g ^ bit), device_id_type=MESH)

    def side_copy(col, part):
        i = sem(col, 0, part)
        step, slot = (-1, 1) if col == 0 else (1, 0)
        return pltpu.make_async_remote_copy(
            src_ref=acc.at[col, 0, cut(part)], dst_ref=beside.at[slot, cut(part)], send_sem=send_sem.at[i],
            recv_sem=recv_sem.at[i], device_id=(b + step, g), device_id_type=MESH)

    odd = [m for m in masks if m & 1]
    for mask in sorted(odd, reverse=True):
        for part in parts:
            for col in cols:
                under(has[col], lambda: grp_copy(col, mask, part).start())
    yield
    held_back = []
    for bit in reversed(grp_bits(groups)):
        kept = [m for m in range(groups) if m % (2 * bit) == 0]

        def settle(mask, col, part):
            def step():
                grp_copy(col, mask | bit, part).wait_recv()
                held = sent.at[col, g ^ mask, cut(part)] if bit == 1 else acc.at[col, mask, cut(part)]
                add_blocks(acc.at[col, mask, cut(part)], held, land.at[col, mask | bit, cut(part)], span)
                if mask and low_bit(mask) == 2 * bit:
                    if col == 1 and 4 * bit == groups:
                        held_back.append((mask, part))
                    else:
                        grp_copy(col, mask, part).start()
                if 2 * bit == groups and col != 1:
                    side_copy(col, part).start()
            under(has[col], step)

        for mask in sorted(kept, reverse=True):
            for part in parts:
                for col in (0, 2):
                    settle(mask, col, part)
                if 2 * bit == groups and part == PARTS // 2 - 1:
                    yield
                    for late, piece in held_back:
                        grp_copy(1, late, piece).start()
            if 2 * bit == groups:
                yield
            for part in parts:
                settle(mask, 1, part)
            yield
    for part in parts:
        for col in (0, 2):
            pl.when(has[opposite[col]])(lambda: side_copy(col, part).wait_recv())
    for part in parts:
        for col in (0, 2):
            pl.when(has[col])(lambda: side_copy(col, part).wait_send())
        for mask in masks:
            for col in cols:
                under(has[col], lambda: grp_copy(col, mask, part).wait_send())


def dot(a, b):
    return jnp.dot(a, b, preferred_element_type=F32)


def clear_edges(near, columns):
    _, _, has = where_am_i(columns)
    for col in (0, 2):
        @pl.when(jnp.logical_not(has[col]))
        def _():
            def clear(h, carry):
                for x in range(near.shape[2]):
                    near[col, h, x] = jnp.zeros(near.shape[3:], near.dtype)
                return carry
            lax.fori_loop(0, near.shape[1], clear, 0)


class Tables:
    def __init__(self, ref, slots, blocks):
        self.ref, self.slots, self.blocks = ref, slots, blocks

    def entry(self, row, slot):
        return self.ref[row * self.slots + slot]

    def first(self, slot):
        return self.entry(0, slot)

    def second(self, slot):
        return self.entry(1, slot), self.entry(2, slot), self.entry(3, slot)

    def flag(self, slot):
        return self.entry(4, slot).astype(F32)

    def before_first(self, slot):
        return self.entry(5, slot)

    def before_second(self, slot):
        return self.entry(6, slot)

    def last_first(self, block):
        return self.ref[7 * self.slots + block]

    def last_second(self, place):
        return self.ref[7 * self.slots + self.blocks + place]


def table_of(pair_list, used, column, blocks, groups):
    slots = pair_list.shape[0]
    index = jnp.arange(slots, dtype=jnp.int32)
    active = index < used
    first = pair_list[:, 0]
    owner = pair_list[:, 1] // blocks
    col, h, x = owner // groups - column + 1, owner % groups, pair_list[:, 1] % blocks
    place = (col * groups + h) * blocks + x

    def latest(match):
        return jnp.max(jnp.where(match, index[None, :], -1), axis=1)

    def chain(key, keys):
        earlier = (key[:, None] == key[None, :]) & active[None, :] & (index[None, :] < index[:, None])
        found = latest(earlier)
        here = latest((jnp.arange(keys, dtype=jnp.int32)[:, None] == key[None, :]) & active[None, :])
        return jnp.where(found < 0, slots, found), jnp.where(here < 0, slots, here)

    before_first, last_first = chain(first, blocks)
    before_second, last_second = chain(place, 3 * groups * blocks)
    return jnp.concatenate([first, col, h, x, active.astype(jnp.int32), before_first, before_second, last_first, last_second])


def fetch(influence, tiles, tile_sem, slot):
    return pltpu.make_async_copy(influence.at[slot], tiles.at[slot], tile_sem.at[slot])


def fill_sent(sent, tables, message):
    groups, blocks = sent.shape[1], sent.shape[2]
    for col in range(3):
        def place(h, carry):
            for x in range(blocks):
                sent[col, h, x] = message[tables.last_second((col * groups + h) * blocks + x)].astype(BF16)
            return carry
        lax.fori_loop(0, groups, place, 0)


def reduced_rows(tables, message, acc, beside, total, columns):
    _, _, has = where_am_i(columns)
    for i in range(total.shape[0]):
        total[i] = message[tables.last_first(i)] + acc[1, 0, i].astype(F32)
    for slot, col in ((0, 0), (1, 2)):
        @pl.when(has[col])
        def _():
            for i in range(total.shape[0]):
                total[i] += beside[slot, i].astype(F32)


def rows_below(count, shape):
    return lax.broadcasted_iota(jnp.int32, shape, 0) < count


def lay_out(kernel_weights, weights, mirror_t):
    kernels, width = kernel_weights.shape[:2]
    for k in range(kernels):
        weights[:, k * width:(k + 1) * width] = kernel_weights[k]
        mirror_t[k * width:(k + 1) * width, :] = kernel_weights[kernels - 1 - k].astype(F32).T.astype(BF16)


def halves(slots, work):
    middle = slots // 2
    for start, end in ((0, middle), (middle, slots)):
        def step(slot, carry):
            work(slot)
            return carry
        yield lambda: lax.fori_loop(start, end, step, 0)


def forward_pass(columns, counts, table, features, influence, kernel_weights, cotangent,
                 activated, upstream, near,
                 weights, mirror_t, mine, tiles, left, right, to_second, to_first, sent,
                 acc, land, beside, total, tile_sem, send_sem, recv_sem, send_sem2, recv_sem2):
    _, g, _ = where_am_i(columns)
    slots, kernels, width = tiles.shape[0], tiles.shape[1], features.shape[2]
    tables = Tables(table, slots, features.shape[0])
    for slot in range(slots):
        fetch(influence, tiles, tile_sem, slot).start()
    for i in range(features.shape[0]):
        rows = features[i].astype(F32)
        rows = jnp.where(rows_below(counts[i], rows.shape), rows, 0.0).astype(BF16)
        mine[i] = rows
        near[1, g, i] = rows
    lay_out(kernel_weights, weights, mirror_t)
    clear_edges(near, columns)
    to_second[slots] = jnp.zeros(to_second.shape[1:], F32)
    to_first[slots] = jnp.zeros(to_first.shape[1:], F32)

    def own_terms(slot):
        fetch(influence, tiles, tile_sem, slot).wait()
        rows_t = mine[tables.first(slot)].astype(F32).T.astype(BF16)
        left[...] = dot(mirror_t[...], rows_t).astype(BF16)
        value = jnp.zeros(to_second.shape[1:][::-1], F32)
        for k in range(kernels):
            value += dot(left[k * width:(k + 1) * width, :], tiles[slot, k])
        to_second[slot] = value.T + to_second[tables.before_second(slot)]

    def near_terms(slot):
        col, h, x = tables.second(slot)
        right[...] = dot(near[col, h, x], weights[...]).astype(BF16)
        value = jnp.zeros(to_first.shape[1:], F32)
        for k in range(kernels):
            value += dot(tiles[slot, k], right[:, k * width:(k + 1) * width])
        to_first[slot] = value + to_first[tables.before_first(slot)]

    greet(columns, near.shape[1])
    work = halves(slots, own_terms)
    steps = spread(near, send_sem, recv_sem, columns)
    next(steps)
    next(work)()
    next(steps)
    next(work)()
    run(steps)
    fill_sent(sent, tables, to_second)
    work = halves(slots, near_terms)
    steps = gather_back(sent, acc, land, beside, send_sem2, recv_sem2, columns)
    next(steps)
    next(steps)
    next(steps)
    next(work)()
    next(steps)
    next(work)()
    run(steps)
    reduced_rows(tables, to_first, acc, beside, total, columns)
    for i in range(total.shape[0]):
        keep = rows_below(counts[i], total.shape[1:])
        pre = jnp.where(keep, total[i], 0.0)
        sig = jax.nn.sigmoid(pre)
        activated[i] = (pre * sig).astype(BF16)
        slope = sig * (1.0 + pre * (1.0 - sig))
        upstream[i] = jnp.where(keep, cotangent[i].astype(F32) * slope, 0.0).astype(BF16)


def sum_weights(scale, terms, out, land, held, low, low_land, mixed, gathered, send_sem, recv_sem, columns):
    b, g, _ = where_am_i(columns)
    groups = terms.shape[0]
    bits = grp_bits(groups)
    base_a, base_b, base_c = groups, groups + columns, groups + 2 * columns
    distances = range(1, columns)

    def copy(src, dst, i, device):
        return pltpu.make_async_remote_copy(
            src_ref=src, dst_ref=dst, send_sem=send_sem.at[i], recv_sem=recv_sem.at[i],
            device_id=device, device_id_type=MESH)

    def halve(mask):
        bit = low_bit(mask)
        if bit == 1:
            return copy(terms.at[g ^ mask], land.at[mask], mask, (b, g ^ bit))
        return copy(low.at[mask], low_land.at[mask], mask, (b, g ^ bit))

    def share(distance):
        peer = lax.rem(b + distance, columns)
        return copy(low.at[0, peer], mixed.at[distance], base_a + distance, (peer, g))

    def tell(distance):
        peer = lax.rem(b + distance, columns)
        return copy(gathered.at[g, b], gathered.at[g, b], base_b + distance, (peer, g))

    def told(distance):
        peer = lax.rem(b + columns - distance, columns)
        return copy(gathered.at[g, b], gathered.at[g, peer], base_b + distance, (peer, g))

    def double(mask):
        piece = gathered.at[g ^ mask ^ low_bit(mask)]
        return copy(piece, piece, base_c + mask, (b, g ^ low_bit(mask)))

    def doubled(mask):
        return copy(gathered.at[g], gathered.at[g ^ mask], base_c + mask, (b, g ^ low_bit(mask)))

    masks = grp_masks(groups)
    for mask in masks:
        if mask & 1:
            halve(mask).start()
    yield
    for bit in reversed(bits):
        for mask in sorted((m for m in range(groups) if m % (2 * bit) == 0), reverse=True):
            halve(mask | bit).wait_recv()
            for n in range(columns):
                if bit == 1:
                    value = terms[g ^ mask, n] + land[mask | 1, n]
                else:
                    value = held[mask, n] + low_land[mask | bit, n].astype(F32)
                held[mask, n] = value
                low[mask, n] = value.astype(BF16)
            if mask and low_bit(mask) == 2 * bit:
                halve(mask).start()
        if 2 * bit == groups:
            for distance in distances:
                share(distance).start()
        yield
    for distance in distances:
        share(distance).wait_recv()
    total = held[0, b]
    for distance in distances:
        total += mixed[distance].astype(F32)
    gathered[g, b] = total.astype(BF16)
    for distance in distances:
        tell(distance).start()
    yield
    for distance in distances:
        told(distance).wait_recv()
    for bit in bits:
        double(bit).start()
    yield
    for mask in masks:
        doubled(mask).wait_recv()
        for bit in bits:
            if bit < low_bit(mask):
                double(mask | bit).start()
        if low_bit(mask) == 2:
            yield
    for mask in masks:
        halve(mask).wait_send()
        double(mask).wait_send()
    for distance in distances:
        share(distance).wait_send()
        tell(distance).wait_send()
    rows = gathered.shape[2]
    shares = out.shape[1] // rows
    for at in range(out.shape[0] * shares):
        piece = gathered[at // columns, at % columns]
        out[at // shares, at % shares * rows:(at % shares + 1) * rows] = piece.astype(F32) * scale


def backward_pass(scale, columns, counts, table, near, upstream, influence, kernel_weights,
                  grad, summed,
                  weights, mirror_t, near_up, tiles, up_t, up_own, grad_near, grad_own, grads, to_second, to_first, sent,
                  acc, land, beside, total, tile_sem, send_sem, recv_sem, send_sem2, recv_sem2,
                  w_land, w_held, w_low, w_low_land, w_mixed, w_gathered, w_send, w_recv):
    _, g, _ = where_am_i(columns)
    slots, kernels, width = tiles.shape[0], tiles.shape[1], upstream.shape[2]
    tables = Tables(table, slots, upstream.shape[0])
    for slot in range(slots):
        fetch(influence, tiles, tile_sem, slot).start()
    for i in range(upstream.shape[0]):
        near_up[1, g, i] = upstream[i]
    lay_out(kernel_weights, weights, mirror_t)
    clear_edges(near_up, columns)
    to_second[slots] = jnp.zeros(to_second.shape[1:], F32)
    to_first[slots] = jnp.zeros(to_first.shape[1:], F32)
    grad_near[...] = jnp.zeros_like(grad_near)
    grad_own[...] = jnp.zeros_like(grad_own)

    def near_terms(slot):
        fetch(influence, tiles, tile_sem, slot).wait()
        col, h, x = tables.second(slot)
        up_first_t = (upstream[tables.first(slot)].astype(F32) * tables.flag(slot)).T.astype(BF16)
        for k in range(kernels):
            up_t[k * width:(k + 1) * width, :] = dot(up_first_t, tiles[slot, k]).astype(BF16)
        grad_near[...] += dot(up_t[...], near[col, h, x])
        to_second[slot] = dot(weights[...], up_t[...]).T + to_second[tables.before_second(slot)]

    def own_terms(slot):
        col, h, x = tables.second(slot)
        up_second = (near_up[col, h, x].astype(F32) * tables.flag(slot)).astype(BF16)
        for k in range(kernels):
            up_own[:, k * width:(k + 1) * width] = dot(tiles[slot, k], up_second).astype(BF16)
        rows_t = near[1, g, tables.first(slot)].astype(F32).T.astype(BF16)
        grad_own[...] += dot(rows_t, up_own[...])
        to_first[slot] = dot(up_own[...], mirror_t[...]) + to_first[tables.before_first(slot)]

    greet(columns, near.shape[1], True)
    work = halves(slots, near_terms)
    steps = spread(near_up, send_sem, recv_sem, columns)
    next(steps)
    next(work)()
    next(steps)
    next(work)()
    run(steps)
    fill_sent(sent, tables, to_second)
    work = halves(slots, own_terms)
    steps = gather_back(sent, acc, land, beside, send_sem2, recv_sem2, columns)
    next(steps)
    next(steps)
    next(work)()
    next(steps)
    next(steps)
    next(work)()
    rows = grads.shape[2]
    shares = width // rows
    for k in range(kernels):
        mirrored = kernels - 1 - k
        value = grad_near[k * width:(k + 1) * width, :].T + grad_own[:, mirrored * width:(mirrored + 1) * width]
        for i in range(shares):
            at = k * shares + i
            grads[at // columns, at % columns] = value[i * rows:(i + 1) * rows]
    for at in range(kernels * shares, grads.shape[0] * columns):
        grads[at // columns, at % columns] = jnp.zeros(grads.shape[2:], F32)
    weight_steps = sum_weights(
        scale, grads, summed, w_land, w_held, w_low, w_low_land, w_mixed, w_gathered, w_send, w_recv, columns)
    next(weight_steps)
    next(weight_steps)
    next(steps)
    next(weight_steps)
    next(steps)
    next(weight_steps)
    run(steps)
    next(weight_steps)
    reduced_rows(tables, to_first, acc, beside, total, columns)
    for i in range(total.shape[0]):
        keep = rows_below(counts[i], total.shape[1:])
        grad[i] = jnp.where(keep, total[i], 0.0).astype(BF16)
    run(weight_steps)


def body(features, point_counts, kernel_weights, influence, pair_list, pair_counts, cotangent):
    blocks, points, width = features.shape
    kernels = kernel_weights.shape[0]
    slots = influence.shape[0]
    columns, groups = lax.axis_size("block"), lax.axis_size("grp")
    spread_shape = (3, groups, blocks, points, width)
    own_shape = (blocks, points, width)
    terms = (kernels * width, points)

    table = table_of(pair_list, pair_counts[0], lax.axis_index("block"), blocks, groups)

    def remote(kernel, collective, ins, outs, scratch, args):
        return pl.pallas_call(
            kernel,
            in_specs=ins,
            out_specs=[VMEM] * len(outs),
            out_shape=outs,
            scratch_shapes=scratch,
            compiler_params=pltpu.CompilerParams(
                collective_id=collective, has_side_effects=True, vmem_limit_bytes=VMEM_BYTES),
        )(*args)

    hbm = pl.BlockSpec(memory_space=pl.ANY)
    dma = pltpu.SemaphoreType.DMA((3 * groups * PARTS,))
    messages = pltpu.VMEM((slots + 1, points, width), F32)
    tiles = pltpu.VMEM(influence.shape, BF16)
    exchange = [
        messages, messages, pltpu.VMEM(spread_shape, BF16),
        pltpu.VMEM(spread_shape, BF16), pltpu.VMEM(spread_shape, BF16),
        pltpu.VMEM((2, *own_shape), BF16), pltpu.VMEM(own_shape, F32),
        pltpu.SemaphoreType.DMA((slots,)), dma, dma, dma, dma]
    laid_out = [pltpu.VMEM((width, kernels * width), BF16), pltpu.VMEM((kernels * width, width), BF16)]
    near_type = jax.ShapeDtypeStruct(spread_shape, BF16)
    own_type = jax.ShapeDtypeStruct(own_shape, BF16)

    activated, upstream, near = remote(
        functools.partial(forward_pass, columns), 0,
        [SMEM, SMEM, VMEM, hbm, VMEM, VMEM], [own_type, own_type, near_type],
        laid_out + [pltpu.VMEM(own_shape, BF16), tiles, pltpu.VMEM(terms, BF16), pltpu.VMEM(terms[::-1], BF16)] + exchange,
        (point_counts, table, features, influence, kernel_weights, cotangent))

    scale = 1.0 / math.sqrt(blocks * points * columns * groups)
    share = 16 * columns * groups
    padded = -(-kernels * width // share) * share // width
    cut = (groups, columns, padded * width // (groups * columns), width)
    w_dma = pltpu.SemaphoreType.DMA((2 * groups + 2 * columns,))
    grad_features, grad_weights = remote(
        functools.partial(backward_pass, scale, columns), 1,
        [SMEM, SMEM, VMEM, VMEM, hbm, VMEM], [own_type, jax.ShapeDtypeStruct(kernel_weights.shape, F32)],
        laid_out + [pltpu.VMEM(spread_shape, BF16), tiles, pltpu.VMEM(terms, BF16), pltpu.VMEM(terms[::-1], BF16),
         pltpu.VMEM((kernels * width, width), F32), pltpu.VMEM((width, kernels * width), F32), pltpu.VMEM(cut, F32)]
        + exchange + [
            pltpu.VMEM(cut, F32), pltpu.VMEM(cut, F32), pltpu.VMEM(cut, BF16), pltpu.VMEM(cut, BF16),
            pltpu.VMEM(cut[1:], BF16), pltpu.VMEM(cut, BF16), w_dma, w_dma],
        (point_counts, table, near, upstream, influence, kernel_weights))
    return (activated, grad_features, grad_weights)


def solution(mesh):
    placed = (
        P(("block", "grp"), None, None),
        P(("block", "grp")),
        P(),
        P(("block", "grp"), None, None, None),
        P(("block", "grp"), None),
        P(("block", "grp")),
        P(("block", "grp"), None, None),
    )
    return jax.shard_map(
        body,
        mesh=mesh,
        in_specs=placed,
        out_specs=(P(("block", "grp"), None, None), P(("block", "grp"), None, None), P()),
        check_vma=False,
    )
```

```python
import functools
import math

import jax
import jax.numpy as jnp
from jax import lax
from jax.experimental import pallas as pl
from jax.experimental.pallas import tpu as pltpu
from jax.sharding import PartitionSpec as P

MESH = pl.DeviceIdType.MESH
F32, BF16 = jnp.float32, jnp.bfloat16
VMEM_BYTES = 56 * 2**20
PARTS = 4
VMEM = pl.BlockSpec(memory_space=pltpu.VMEM)
SMEM = pl.BlockSpec(memory_space=pltpu.SMEM)


def low_bit(mask):
    return mask & -mask


def grp_masks(groups):
    return sorted(range(1, groups), key=lambda m: (-low_bit(m), m))


def grp_bits(groups):
    return [1 << i for i in reversed(range(groups.bit_length() - 1))]


def where_am_i(columns):
    b, g = lax.axis_index("block"), lax.axis_index("grp")
    return b, g, {0: b > 0, 1: None, 2: b < columns - 1}


def under(condition, action):
    if condition is None:
        action()
    else:
        pl.when(condition)(action)


def greet(columns, groups, whole_axis=False):
    b, g, has = where_am_i(columns)
    barrier = pltpu.get_barrier_semaphore()
    peers = len(grp_bits(groups))
    for bit in grp_bits(groups):
        pl.semaphore_signal(barrier, inc=1, device_id=(b, g ^ bit), device_id_type=MESH)
    if whole_axis:
        for distance in range(1, columns):
            pl.semaphore_signal(
                barrier, inc=1, device_id=(lax.rem(b + distance, columns), g), device_id_type=MESH)
        peers = peers + columns - 1
    else:
        for side, step in ((0, -1), (2, 1)):
            @pl.when(has[side])
            def _():
                pl.semaphore_signal(barrier, inc=1, device_id=(b + step, g), device_id_type=MESH)
        peers = peers + has[0].astype(jnp.int32) + has[2].astype(jnp.int32)
    pl.semaphore_wait(barrier, peers)


def spread(near, send_sem, recv_sem, columns):
    b, g, has = where_am_i(columns)
    groups, blocks = near.shape[1], near.shape[2]
    span = blocks // PARTS
    opposite = {0: 2, 2: 0}

    def at(col, mask, part):
        return near.at[col, g ^ mask, pl.ds(part * span, span)]

    def sem(col, mask, part):
        return (col * groups + mask) * PARTS + part

    def side_copy(col, part, mask=0):
        i = sem(col, mask, part)
        step = 1 if col == 0 else -1
        return pltpu.make_async_remote_copy(
            src_ref=at(1, mask, part), dst_ref=at(col, mask, part), send_sem=send_sem.at[i],
            recv_sem=recv_sem.at[i], device_id=(b + step, g), device_id_type=MESH)

    def grp_copy(col, mask, part):
        bit = low_bit(mask)
        i = sem(col, mask, part)
        return pltpu.make_async_remote_copy(
            src_ref=at(col, mask ^ bit, part), dst_ref=at(col, mask ^ bit, part), send_sem=send_sem.at[i],
            recv_sem=recv_sem.at[i], device_id=(b, g ^ bit), device_id_type=MESH)

    def arrival(col, mask, part):
        bit = low_bit(mask)
        i = sem(col, mask, part)
        return pltpu.make_async_remote_copy(
            src_ref=at(col, mask ^ bit, part), dst_ref=at(col, mask, part), send_sem=send_sem.at[i],
            recv_sem=recv_sem.at[i], device_id=(b, g ^ bit), device_id_type=MESH)

    top, turned = groups // 2, PARTS - 1

    def detour(col, mask, part):
        return col != 1 and mask == top and part == turned

    def forward(col, mask, part):
        for bit in grp_bits(groups):
            if (mask == 0 or bit < low_bit(mask)) and not detour(col, mask | bit, part):
                grp_copy(col, mask | bit, part).start()

    parts = range(PARTS)
    forward(1, 0, turned)
    for part in parts:
        for col in (0, 2):
            pl.when(has[opposite[col]])(lambda: side_copy(col, part).start())
        if part != turned:
            forward(1, 0, part)
    yield
    if top:
        arrival(1, top, turned).wait_recv()
        for col in (0, 2):
            pl.when(has[opposite[col]])(lambda: side_copy(col, turned, top).start())
        forward(1, top, turned)
    for part in parts:
        for col in (0, 2):
            @pl.when(has[col])
            def _():
                side_copy(col, part).wait_recv()
                forward(col, 0, part)
    yield
    masks = grp_masks(groups)
    for mask in masks:
        for part in parts:
            for col in (1, 0, 2):
                def step():
                    if detour(col, mask, part):
                        side_copy(col, part, mask).wait_recv()
                    else:
                        arrival(col, mask, part).wait_recv()
                    forward(col, mask, part)
                if (col, mask, part) != (1, top, turned):
                    under(has[col], step)
    for part in parts:
        for col in (0, 2):
            pl.when(has[opposite[col]])(lambda: side_copy(col, part).wait_send())
    for mask in masks:
        for part in parts:
            for col in (0, 1, 2):
                if detour(col, mask, part):
                    pl.when(has[opposite[col]])(lambda: side_copy(col, part, mask).wait_send())
                else:
                    under(has[col], lambda: grp_copy(col, mask, part).wait_send())


def run(*steps):
    for _ in zip(*steps):
        pass
    for step in steps:
        for _ in step:
            pass


def add_blocks(out, one, two, span):
    for i in range(span):
        out[i] = (one[i].astype(F32) + two[i].astype(F32)).astype(BF16)


def gather_back(sent, acc, land, beside, send_sem, recv_sem, columns):
    b, g, has = where_am_i(columns)
    groups, blocks = sent.shape[1], sent.shape[2]
    span = blocks // PARTS
    opposite = {0: 2, 2: 0}
    cols = (0, 2, 1)
    parts = range(PARTS)
    masks = grp_masks(groups)

    def cut(part):
        return pl.ds(part * span, span)

    def sem(col, mask, part):
        return (col * groups + mask) * PARTS + part

    def grp_copy(col, mask, part):
        bit = low_bit(mask)
        i = sem(col, mask, part)
        src = sent.at[col, g ^ mask, cut(part)] if bit == 1 else acc.at[col, mask, cut(part)]
        return pltpu.make_async_remote_copy(
            src_ref=src, dst_ref=land.at[col, mask, cut(part)], send_sem=send_sem.at[i],
            recv_sem=recv_sem.at[i], device_id=(b, g ^ bit), device_id_type=MESH)

    def side_copy(col, part):
        i = sem(col, 0, part)
        step, slot = (-1, 1) if col == 0 else (1, 0)
        return pltpu.make_async_remote_copy(
            src_ref=acc.at[col, 0, cut(part)], dst_ref=beside.at[slot, cut(part)], send_sem=send_sem.at[i],
            recv_sem=recv_sem.at[i], device_id=(b + step, g), device_id_type=MESH)

    odd = [m for m in masks if m & 1]
    for mask in sorted(odd, reverse=True):
        for part in parts:
            for col in cols:
                under(has[col], lambda: grp_copy(col, mask, part).start())
    yield
    held_back = []
    for bit in reversed(grp_bits(groups)):
        kept = [m for m in range(groups) if m % (2 * bit) == 0]

        def settle(mask, col, part):
            def step():
                grp_copy(col, mask | bit, part).wait_recv()
                held = sent.at[col, g ^ mask, cut(part)] if bit == 1 else acc.at[col, mask, cut(part)]
                add_blocks(acc.at[col, mask, cut(part)], held, land.at[col, mask | bit, cut(part)], span)
                if mask and low_bit(mask) == 2 * bit:
                    if col == 1 and 4 * bit == groups:
                        held_back.append((mask, part))
                    else:
                        grp_copy(col, mask, part).start()
                if 2 * bit == groups and col != 1:
                    side_copy(col, part).start()
            under(has[col], step)

        for mask in sorted(kept, reverse=True):
            for part in parts:
                for col in (0, 2):
                    settle(mask, col, part)
                if 2 * bit == groups and part == PARTS // 2 - 1:
                    yield
                    for late, piece in held_back:
                        grp_copy(1, late, piece).start()
            if 2 * bit == groups:
                yield
            for part in parts:
                settle(mask, 1, part)
            yield
    for part in parts:
        for col in (0, 2):
            pl.when(has[opposite[col]])(lambda: side_copy(col, part).wait_recv())
    for part in parts:
        for col in (0, 2):
            pl.when(has[col])(lambda: side_copy(col, part).wait_send())
        for mask in masks:
            for col in cols:
                under(has[col], lambda: grp_copy(col, mask, part).wait_send())


def dot(a, b):
    return jnp.dot(a, b, preferred_element_type=F32)


def clear_edges(near, columns):
    _, _, has = where_am_i(columns)
    for col in (0, 2):
        @pl.when(jnp.logical_not(has[col]))
        def _():
            def clear(h, carry):
                for x in range(near.shape[2]):
                    near[col, h, x] = jnp.zeros(near.shape[3:], near.dtype)
                return carry
            lax.fori_loop(0, near.shape[1], clear, 0)


class Tables:
    def __init__(self, ref, slots, blocks):
        self.ref, self.slots, self.blocks = ref, slots, blocks

    def entry(self, row, slot):
        return self.ref[row * self.slots + slot]

    def first(self, slot):
        return self.entry(0, slot)

    def second(self, slot):
        return self.entry(1, slot), self.entry(2, slot), self.entry(3, slot)

    def flag(self, slot):
        return self.entry(4, slot).astype(F32)

    def before_first(self, slot):
        return self.entry(5, slot)

    def before_second(self, slot):
        return self.entry(6, slot)

    def last_first(self, block):
        return self.ref[7 * self.slots + block]

    def last_second(self, place):
        return self.ref[7 * self.slots + self.blocks + place]


def table_of(pair_list, used, column, blocks, groups):
    slots = pair_list.shape[0]
    index = jnp.arange(slots, dtype=jnp.int32)
    active = index < used
    first = pair_list[:, 0]
    owner = pair_list[:, 1] // blocks
    col, h, x = owner // groups - column + 1, owner % groups, pair_list[:, 1] % blocks
    place = (col * groups + h) * blocks + x

    def latest(match):
        return jnp.max(jnp.where(match, index[None, :], -1), axis=1)

    def chain(key, keys):
        earlier = (key[:, None] == key[None, :]) & active[None, :] & (index[None, :] < index[:, None])
        found = latest(earlier)
        here = latest((jnp.arange(keys, dtype=jnp.int32)[:, None] == key[None, :]) & active[None, :])
        return jnp.where(found < 0, slots, found), jnp.where(here < 0, slots, here)

    before_first, last_first = chain(first, blocks)
    before_second, last_second = chain(place, 3 * groups * blocks)
    return jnp.concatenate([first, col, h, x, active.astype(jnp.int32), before_first, before_second, last_first, last_second])


def fetch(influence, tiles, tile_sem, slot):
    return pltpu.make_async_copy(influence.at[slot], tiles.at[slot], tile_sem.at[slot])


def fill_sent(sent, tables, message):
    groups, blocks = sent.shape[1], sent.shape[2]
    for col in range(3):
        def place(h, carry):
            for x in range(blocks):
                sent[col, h, x] = message[tables.last_second((col * groups + h) * blocks + x)].astype(BF16)
            return carry
        lax.fori_loop(0, groups, place, 0)


def reduced_rows(tables, message, acc, beside, total, columns):
    _, _, has = where_am_i(columns)
    for i in range(total.shape[0]):
        total[i] = message[tables.last_first(i)] + acc[1, 0, i].astype(F32)
    for slot, col in ((0, 0), (1, 2)):
        @pl.when(has[col])
        def _():
            for i in range(total.shape[0]):
                total[i] += beside[slot, i].astype(F32)


def rows_below(count, shape):
    return lax.broadcasted_iota(jnp.int32, shape, 0) < count


def lay_out(kernel_weights, weights, mirror_t):
    kernels, width = kernel_weights.shape[:2]
    for k in range(kernels):
        weights[:, k * width:(k + 1) * width] = kernel_weights[k]
        mirror_t[k * width:(k + 1) * width, :] = kernel_weights[kernels - 1 - k].astype(F32).T.astype(BF16)


def halves(slots, work):
    middle = slots // 2
    for start, end in ((0, middle), (middle, slots)):
        def step(slot, carry):
            work(slot)
            return carry
        yield lambda: lax.fori_loop(start, end, step, 0)


def forward_pass(columns, counts, table, features, influence, kernel_weights, cotangent,
                 activated, upstream, near,
                 weights, mirror_t, mine, tiles, left, right, to_second, to_first, sent,
                 acc, land, beside, total, tile_sem, send_sem, recv_sem, send_sem2, recv_sem2):
    _, g, _ = where_am_i(columns)
    slots, kernels, width = tiles.shape[0], tiles.shape[1], features.shape[2]
    tables = Tables(table, slots, features.shape[0])
    for slot in range(slots):
        fetch(influence, tiles, tile_sem, slot).start()
    for i in range(features.shape[0]):
        rows = features[i].astype(F32)
        rows = jnp.where(rows_below(counts[i], rows.shape), rows, 0.0).astype(BF16)
        mine[i] = rows
        near[1, g, i] = rows
    lay_out(kernel_weights, weights, mirror_t)
    clear_edges(near, columns)
    to_second[slots] = jnp.zeros(to_second.shape[1:], F32)
    to_first[slots] = jnp.zeros(to_first.shape[1:], F32)

    def own_terms(slot):
        fetch(influence, tiles, tile_sem, slot).wait()
        rows_t = mine[tables.first(slot)].astype(F32).T.astype(BF16)
        left[...] = dot(mirror_t[...], rows_t).astype(BF16)
        value = jnp.zeros(to_second.shape[1:][::-1], F32)
        for k in range(kernels):
            value += dot(left[k * width:(k + 1) * width, :], tiles[slot, k])
        to_second[slot] = value.T + to_second[tables.before_second(slot)]

    def near_terms(slot):
        col, h, x = tables.second(slot)
        right[...] = dot(near[col, h, x], weights[...]).astype(BF16)
        value = jnp.zeros(to_first.shape[1:], F32)
        for k in range(kernels):
            value += dot(tiles[slot, k], right[:, k * width:(k + 1) * width])
        to_first[slot] = value + to_first[tables.before_first(slot)]

    greet(columns, near.shape[1])
    work = halves(slots, own_terms)
    steps = spread(near, send_sem, recv_sem, columns)
    next(steps)
    next(work)()
    next(steps)
    next(work)()
    run(steps)
    fill_sent(sent, tables, to_second)
    work = halves(slots, near_terms)
    steps = gather_back(sent, acc, land, beside, send_sem2, recv_sem2, columns)
    next(steps)
    next(steps)
    next(steps)
    next(work)()
    next(steps)
    next(work)()
    run(steps)
    reduced_rows(tables, to_first, acc, beside, total, columns)
    for i in range(total.shape[0]):
        keep = rows_below(counts[i], total.shape[1:])
        pre = jnp.where(keep, total[i], 0.0)
        sig = jax.nn.sigmoid(pre)
        activated[i] = (pre * sig).astype(BF16)
        slope = sig * (1.0 + pre * (1.0 - sig))
        upstream[i] = jnp.where(keep, cotangent[i].astype(F32) * slope, 0.0).astype(BF16)


def sum_weights(scale, terms, out, land, held, low, low_land, mixed, gathered, send_sem, recv_sem, columns):
    b, g, _ = where_am_i(columns)
    groups = terms.shape[0]
    bits = grp_bits(groups)
    base_a, base_b, base_c = groups, groups + columns, groups + 2 * columns
    distances = range(1, columns)

    def copy(src, dst, i, device):
        return pltpu.make_async_remote_copy(
            src_ref=src, dst_ref=dst, send_sem=send_sem.at[i], recv_sem=recv_sem.at[i],
            device_id=device, device_id_type=MESH)

    def halve(mask):
        bit = low_bit(mask)
        if bit == 1:
            return copy(terms.at[g ^ mask], land.at[mask], mask, (b, g ^ bit))
        return copy(low.at[mask], low_land.at[mask], mask, (b, g ^ bit))

    def share(distance):
        peer = lax.rem(b + distance, columns)
        return copy(low.at[0, peer], mixed.at[distance], base_a + distance, (peer, g))

    def tell(distance):
        peer = lax.rem(b + distance, columns)
        return copy(gathered.at[g, b], gathered.at[g, b], base_b + distance, (peer, g))

    def told(distance):
        peer = lax.rem(b + columns - distance, columns)
        return copy(gathered.at[g, b], gathered.at[g, peer], base_b + distance, (peer, g))

    def double(mask):
        piece = gathered.at[g ^ mask ^ low_bit(mask)]
        return copy(piece, piece, base_c + mask, (b, g ^ low_bit(mask)))

    def doubled(mask):
        return copy(gathered.at[g], gathered.at[g ^ mask], base_c + mask, (b, g ^ low_bit(mask)))

    masks = grp_masks(groups)
    for mask in masks:
        if mask & 1:
            halve(mask).start()
    yield
    for bit in reversed(bits):
        for mask in sorted((m for m in range(groups) if m % (2 * bit) == 0), reverse=True):
            halve(mask | bit).wait_recv()
            for n in range(columns):
                if bit == 1:
                    value = terms[g ^ mask, n] + land[mask | 1, n]
                else:
                    value = held[mask, n] + low_land[mask | bit, n].astype(F32)
                held[mask, n] = value
                low[mask, n] = value.astype(BF16)
            if mask and low_bit(mask) == 2 * bit:
                halve(mask).start()
        if 2 * bit == groups:
            for distance in distances:
                share(distance).start()
        yield
    for distance in distances:
        share(distance).wait_recv()
    total = held[0, b]
    for distance in distances:
        total += mixed[distance].astype(F32)
    gathered[g, b] = total.astype(BF16)
    for distance in distances:
        tell(distance).start()
    yield
    for distance in distances:
        told(distance).wait_recv()
    for bit in bits:
        double(bit).start()
    yield
    for mask in masks:
        doubled(mask).wait_recv()
        for bit in bits:
            if bit < low_bit(mask):
                double(mask | bit).start()
        if low_bit(mask) == 2:
            yield
    for mask in masks:
        halve(mask).wait_send()
        double(mask).wait_send()
    for distance in distances:
        share(distance).wait_send()
        tell(distance).wait_send()
    rows = gathered.shape[2]
    shares = out.shape[1] // rows
    for at in range(out.shape[0] * shares):
        piece = gathered[at // columns, at % columns]
        out[at // shares, at % shares * rows:(at % shares + 1) * rows] = piece.astype(F32) * scale


def backward_pass(scale, columns, counts, table, near, upstream, influence, kernel_weights,
                  grad, summed,
                  weights, mirror_t, near_up, tiles, up_t, up_own, grad_near, grad_own, grads, to_second, to_first, sent,
                  acc, land, beside, total, tile_sem, send_sem, recv_sem, send_sem2, recv_sem2,
                  w_land, w_held, w_low, w_low_land, w_mixed, w_gathered, w_send, w_recv):
    _, g, _ = where_am_i(columns)
    slots, kernels, width = tiles.shape[0], tiles.shape[1], upstream.shape[2]
    tables = Tables(table, slots, upstream.shape[0])
    for slot in range(slots):
        fetch(influence, tiles, tile_sem, slot).start()
    for i in range(upstream.shape[0]):
        near_up[1, g, i] = upstream[i]
    lay_out(kernel_weights, weights, mirror_t)
    clear_edges(near_up, columns)
    to_second[slots] = jnp.zeros(to_second.shape[1:], F32)
    to_first[slots] = jnp.zeros(to_first.shape[1:], F32)
    grad_near[...] = jnp.zeros_like(grad_near)
    grad_own[...] = jnp.zeros_like(grad_own)

    def near_terms(slot):
        fetch(influence, tiles, tile_sem, slot).wait()
        col, h, x = tables.second(slot)
        up_first_t = (upstream[tables.first(slot)].astype(F32) * tables.flag(slot)).T.astype(BF16)
        for k in range(kernels):
            up_t[k * width:(k + 1) * width, :] = dot(up_first_t, tiles[slot, k]).astype(BF16)
        grad_near[...] += dot(up_t[...], near[col, h, x])
        to_second[slot] = dot(weights[...], up_t[...]).T + to_second[tables.before_second(slot)]

    def own_terms(slot):
        col, h, x = tables.second(slot)
        up_second = (near_up[col, h, x].astype(F32) * tables.flag(slot)).astype(BF16)
        for k in range(kernels):
            up_own[:, k * width:(k + 1) * width] = dot(tiles[slot, k], up_second).astype(BF16)
        rows_t = near[1, g, tables.first(slot)].astype(F32).T.astype(BF16)
        grad_own[...] += dot(rows_t, up_own[...])
        to_first[slot] = dot(up_own[...], mirror_t[...]) + to_first[tables.before_first(slot)]

    greet(columns, near.shape[1], True)
    work = halves(slots, near_terms)
    steps = spread(near_up, send_sem, recv_sem, columns)
    next(steps)
    next(work)()
    next(steps)
    next(work)()
    run(steps)
    fill_sent(sent, tables, to_second)
    work = halves(slots, own_terms)
    steps = gather_back(sent, acc, land, beside, send_sem2, recv_sem2, columns)
    next(steps)
    next(steps)
    next(work)()
    next(steps)
    next(steps)
    next(work)()
    rows = grads.shape[2]
    shares = width // rows
    for k in range(kernels):
        mirrored = kernels - 1 - k
        value = grad_near[k * width:(k + 1) * width, :].T + grad_own[:, mirrored * width:(mirrored + 1) * width]
        for i in range(shares):
            at = k * shares + i
            grads[at // columns, at % columns] = value[i * rows:(i + 1) * rows]
    for at in range(kernels * shares, grads.shape[0] * columns):
        grads[at // columns, at % columns] = jnp.zeros(grads.shape[2:], F32)
    weight_steps = sum_weights(
        scale, grads, summed, w_land, w_held, w_low, w_low_land, w_mixed, w_gathered, w_send, w_recv, columns)
    next(weight_steps)
    next(weight_steps)
    next(steps)
    next(weight_steps)
    next(steps)
    next(weight_steps)
    run(steps)
    next(weight_steps)
    reduced_rows(tables, to_first, acc, beside, total, columns)
    for i in range(total.shape[0]):
        keep = rows_below(counts[i], total.shape[1:])
        grad[i] = jnp.where(keep, total[i], 0.0).astype(BF16)
    run(weight_steps)


def body(features, point_counts, kernel_weights, influence, pair_list, pair_counts, cotangent):
    blocks, points, width = features.shape
    kernels = kernel_weights.shape[0]
    slots = influence.shape[0]
    columns, groups = lax.axis_size("block"), lax.axis_size("grp")
    spread_shape = (3, groups, blocks, points, width)
    own_shape = (blocks, points, width)
    terms = (kernels * width, points)

    table = table_of(pair_list, pair_counts[0], lax.axis_index("block"), blocks, groups)

    def remote(kernel, collective, ins, outs, scratch, args):
        return pl.pallas_call(
            kernel,
            in_specs=ins,
            out_specs=[VMEM] * len(outs),
            out_shape=outs,
            scratch_shapes=scratch,
            compiler_params=pltpu.CompilerParams(
                collective_id=collective, has_side_effects=True, vmem_limit_bytes=VMEM_BYTES),
        )(*args)

    hbm = pl.BlockSpec(memory_space=pl.ANY)
    dma = pltpu.SemaphoreType.DMA((3 * groups * PARTS,))
    messages = pltpu.VMEM((slots + 1, points, width), F32)
    tiles = pltpu.VMEM(influence.shape, BF16)
    exchange = [
        messages, messages, pltpu.VMEM(spread_shape, BF16),
        pltpu.VMEM(spread_shape, BF16), pltpu.VMEM(spread_shape, BF16),
        pltpu.VMEM((2, *own_shape), BF16), pltpu.VMEM(own_shape, F32),
        pltpu.SemaphoreType.DMA((slots,)), dma, dma, dma, dma]
    laid_out = [pltpu.VMEM((width, kernels * width), BF16), pltpu.VMEM((kernels * width, width), BF16)]
    near_type = jax.ShapeDtypeStruct(spread_shape, BF16)
    own_type = jax.ShapeDtypeStruct(own_shape, BF16)

    activated, upstream, near = remote(
        functools.partial(forward_pass, columns), 0,
        [SMEM, SMEM, VMEM, hbm, VMEM, VMEM], [own_type, own_type, near_type],
        laid_out + [pltpu.VMEM(own_shape, BF16), tiles, pltpu.VMEM(terms, BF16), pltpu.VMEM(terms[::-1], BF16)] + exchange,
        (point_counts, table, features, influence, kernel_weights, cotangent))

    scale = 1.0 / math.sqrt(blocks * points * columns * groups)
    share = 16 * columns * groups
    padded = -(-kernels * width // share) * share // width
    cut = (groups, columns, padded * width // (groups * columns), width)
    w_dma = pltpu.SemaphoreType.DMA((2 * groups + 2 * columns,))
    grad_features, grad_weights = remote(
        functools.partial(backward_pass, scale, columns), 1,
        [SMEM, SMEM, VMEM, VMEM, hbm, VMEM], [own_type, jax.ShapeDtypeStruct(kernel_weights.shape, F32)],
        laid_out + [pltpu.VMEM(spread_shape, BF16), tiles, pltpu.VMEM(terms, BF16), pltpu.VMEM(terms[::-1], BF16),
         pltpu.VMEM((kernels * width, width), F32), pltpu.VMEM((width, kernels * width), F32), pltpu.VMEM(cut, F32)]
        + exchange + [
            pltpu.VMEM(cut, F32), pltpu.VMEM(cut, F32), pltpu.VMEM(cut, BF16), pltpu.VMEM(cut, BF16),
            pltpu.VMEM(cut[1:], BF16), pltpu.VMEM(cut, BF16), w_dma, w_dma],
        (point_counts, table, near, upstream, influence, kernel_weights))
    return (activated, grad_features, grad_weights)


def solution(mesh):
    placed = (
        P(("block", "grp"), None, None),
        P(("block", "grp")),
        P(),
        P(("block", "grp"), None, None, None),
        P(("block", "grp"), None),
        P(("block", "grp")),
        P(("block", "grp"), None, None),
    )
    return jax.shard_map(
        body,
        mesh=mesh,
        in_specs=placed,
        out_specs=(P(("block", "grp"), None, None), P(("block", "grp"), None, None), P()),
        check_vma=False,
    )
```
